32 devices in a mesh: ctx: 16 (over z, x, core), head: 2 (over y).
Axes of the slice: x: 2, y: 2, z: 4, core: 2. Of those that a mesh axis runs over, the one named last changes fastest.
Arguments:
- queries: bfloat16 [4096, 4, 8, 128], P('ctx', 'head'), may hold values from -6 to 6
- keys: bfloat16 [4096, 8, 128], P('ctx'), may hold values from -6 to 6
- values: bfloat16 [4096, 8, 128], P('ctx'), may hold values from -6 to 6
- dout: bfloat16 [4096, 4, 8, 128], P('ctx', 'head'), may hold values from -24 to 24
- signs: int32 [2, 128, 32], replicated, may hold values from 0 to 1
Outputs:
- dq: bfloat16 [4096, 4, 8, 128], P('ctx', 'head')
- dk: bfloat16 [4096, 8, 128], P('ctx', 'head')
- dv: bfloat16 [4096, 8, 128], P('ctx', 'head')
The draws below stay inside these ranges and needn't reach their ends.
All inputs are finite; a program needn't handle non-finite values.
Results may differ from the reference program's by a relative error of at most 0.0075.
Values may be sent and summed in bfloat16 or wider, within the bound.
A program may use at most 128 MiB of HBM per device.

```python
import jax
import jax.numpy as jnp
from jax import lax

HD = 128
KVH = 8
GROUP = 4
SKETCH = 32
FEAT = 1024
TOK_DEV = 256
TOKENS = 4096


def set_ends(result, stream_key, smallest, top_value):
    dims = result.shape
    place = [jax.random.randint(jax.random.fold_in(stream_key, axis), (), 0, dims[axis]) for axis in range(len(dims))]
    result = result.at[tuple(place)].set(smallest)
    longest = dims.index(max(dims))
    place[longest] = (place[longest] + 1) % dims[longest]
    return result.at[tuple(place)].set(top_value)


def block_scale(stream_key, shape, split, smallest, largest):
    def one(axis_at, blocks):
        heights = jax.random.uniform(jax.random.fold_in(jax.random.fold_in(stream_key, 6), axis_at), (blocks,), jnp.float32, smallest / len(split), largest / len(split))
        return jnp.repeat(jnp.exp(heights), shape[axis_at] // blocks).reshape((-1,) + (1,) * (len(shape) - axis_at - 1))

    gain = one(*split[0])
    for cut in split[1:]:
        gain = gain * one(*cut)
    return gain


def bell_draw(stream_key, shape, scale, reach, cuts=(), dtype=jnp.bfloat16):
    result = jax.random.normal(stream_key, shape, jnp.float32) * scale
    if len(cuts) > 0:
        result = block_scale(stream_key, shape, cuts, -0.22, 0.18) * result
    return jnp.clip(result, min=-reach, max=reach).astype(dtype)


def setup_inputs(seed: int = 0) -> dict:
    streams_of = jax.random.split(jax.random.key(seed), 6)
    queries = bell_draw(streams_of[0], (TOKENS, GROUP, KVH, HD), 1.0, 6.0, ((0, 16), (1, 2)))
    keys = bell_draw(streams_of[1], (TOKENS, KVH, HD), 1.0, 6.0, ((0, 16),))
    values = bell_draw(streams_of[2], (TOKENS, KVH, HD), 1.0, 6.0, ((0, 16),))
    dout = bell_draw(streams_of[3], (TOKENS, GROUP, KVH, HD), 4.0, 24.0, ((0, 16), (1, 2)))
    signs = set_ends(jax.random.randint(streams_of[4], (2, HD, SKETCH), 0, 2), jax.random.fold_in(streams_of[4], 1), 0, 1).astype(jnp.int32)
    return dict(queries=queries, keys=keys, values=values, dout=dout, signs=signs)


highest = lax.Precision.HIGHEST


def matmul(pattern, first, second):
    return jnp.einsum(pattern, first.astype(jnp.float32), second.astype(jnp.float32), precision=highest)


def sketch_parts(tokens, projector, pattern):
    inverse = tokens.shape[-1] ** -0.5
    sketch_one = matmul(pattern, tokens, projector[0]) * inverse
    sketch_two = matmul(pattern, tokens, projector[1]) * inverse
    return sketch_one, sketch_two


def features(sketch_one, sketch_two):
    width = sketch_one.shape[-1]
    sketch = sketch_one * sketch_two
    outer = sketch[..., :, None] * sketch[..., None, :] * (1.0 / width)
    return outer.reshape(sketch.shape[:-1] + (width * width,)).astype(jnp.bfloat16)


def feature_back(cotangent, sketch_one, sketch_two, proj_wide):
    width = sketch_one.shape[-1]
    sketch = sketch_one * sketch_two
    square = cotangent.reshape(cotangent.shape[:-1] + (width, width))
    dsketch = (jnp.einsum('...ab,...b->...a', square, sketch, precision=highest) + jnp.einsum('...ab,...a->...b', square, sketch, precision=highest)) * (1.0 / width)
    back_one = jnp.einsum('...f,df->...d', dsketch * sketch_two, proj_wide[0], precision=highest)
    back_two = jnp.einsum('...f,df->...d', dsketch * sketch_one, proj_wide[1], precision=highest)
    return (back_one + back_two) * proj_wide.shape[1] ** -0.5


def head_step(inputs):
    key_feat, value_head, state_in, total_in, query_feat, grad_out = inputs
    length = key_feat.shape[0]
    causal = lax.broadcasted_iota(jnp.int32, (length, length), 0) >= lax.broadcasted_iota(jnp.int32, (length, length), 1)

    def member(query_one, grad_one):
        scores = jnp.where(causal, matmul('if,jf->ij', query_one, key_feat), 0.0)
        weights = scores.astype(jnp.bfloat16)
        query_wide = query_one.astype(jnp.float32)
        numerator = matmul('ij,jd->id', weights, value_head) + jnp.dot(query_wide, state_in, precision=highest)
        denominator = 1.0 + jnp.sum(scores, 1) + jnp.dot(query_wide, total_in, precision=highest)
        output_rows = numerator / denominator[:, None]
        grad_rows = grad_one.astype(jnp.float32) / denominator[:, None]
        grad_low = grad_rows.astype(jnp.bfloat16)
        correction = -jnp.sum(grad_rows * output_rows, 1)
        dscores = jnp.where(causal, matmul('id,jd->ij', grad_low, value_head) + correction[:, None], 0.0).astype(jnp.bfloat16)
        grad_qfeat = matmul('ij,jf->if', dscores, key_feat) + jnp.dot(grad_rows, state_in.T, precision=highest) + correction[:, None] * total_in[None, :]
        grad_kfeat = matmul('ij,if->jf', dscores, query_one)
        grad_value = matmul('ij,id->jd', weights, grad_low)
        suffix_part = matmul('if,id->fd', query_one, grad_low)
        suffix_sum = jnp.dot(correction, query_wide, precision=highest)
        return grad_qfeat, grad_kfeat, grad_value, suffix_part, suffix_sum

    results = jax.vmap(member)(query_feat, grad_out)
    return results[0], jnp.sum(results[1], 0), jnp.sum(results[2], 0), results[3], results[4]


def add_states(running_sum, block_term):
    updated = (running_sum[0] + block_term[0], running_sum[1] + block_term[1])
    return updated, running_sum


def reference(queries, keys, values, dout, signs):
    projector = (2 * signs - 1).astype(jnp.bfloat16)
    proj_wide = projector.astype(jnp.float32)
    blocks = TOKENS // TOK_DEV
    query_blocks = queries.reshape(blocks, TOK_DEV, GROUP, KVH, HD)
    key_blocks = keys.reshape(blocks, TOK_DEV, KVH, HD)
    value_blocks = values.reshape(blocks, TOK_DEV, KVH, HD)
    grad_blocks = dout.reshape(blocks, TOK_DEV, GROUP, KVH, HD)

    def block_totals(block_pair):
        key_blk, value_blk = block_pair
        sketch_one, sketch_two = sketch_parts(key_blk, projector, 'thd,df->htf')
        key_feat = features(sketch_one, sketch_two)
        value_heads = value_blk.transpose(1, 0, 2)
        return matmul('htf,htd->hfd', key_feat, value_heads), jnp.sum(key_feat.astype(jnp.float32), 1)

    totals = lax.map(block_totals, (key_blocks, value_blocks))
    start_states = (jnp.zeros((KVH, FEAT, HD), jnp.float32), jnp.zeros((KVH, FEAT), jnp.float32))
    final_state, prefix = lax.scan(add_states, start_states, totals)

    def forward_block(block_items):
        query_blk, key_blk, value_blk, grad_blk, state_in, total_in = block_items
        key_one, key_two = sketch_parts(key_blk, projector, 'thd,df->htf')
        key_feat = features(key_one, key_two)
        query_one, query_two = sketch_parts(query_blk, projector, 'tmhd,df->hmtf')
        query_feat = features(query_one, query_two)
        value_heads = value_blk.transpose(1, 0, 2)
        grad_heads = grad_blk.transpose(2, 1, 0, 3)
        grad_qfeat, grad_kfeat, grad_value, suffix_part, suffix_sum = lax.map(head_step, (key_feat, value_heads, state_in, total_in, query_feat, grad_heads))
        query_grad = feature_back(grad_qfeat, query_one, query_two, proj_wide)
        return query_grad.transpose(2, 1, 0, 3).astype(jnp.bfloat16), grad_kfeat, grad_value, suffix_part, suffix_sum

    dq_blocks, grad_kfeat, grad_value, suffix_part, suffix_sum = lax.map(forward_block, (query_blocks, key_blocks, value_blocks, grad_blocks, prefix[0], prefix[1]))
    start_suffix = (jnp.zeros((KVH, GROUP, FEAT, HD), jnp.float32), jnp.zeros((KVH, GROUP, FEAT), jnp.float32))
    final_suffix, suffix = lax.scan(add_states, start_suffix, (suffix_part, suffix_sum), reverse=True)

    def backward_block(block_items):
        key_blk, value_blk, grad_kblk, grad_vblk, suffix_state, suffix_total = block_items
        key_one, key_two = sketch_parts(key_blk, projector, 'thd,df->htf')
        key_feat = features(key_one, key_two)
        value_heads = value_blk.transpose(1, 0, 2)
        merged_state = jnp.sum(suffix_state, 1)
        merged_total = jnp.sum(suffix_total, 1)
        kfeat_total = grad_kblk + jnp.einsum('htd,hfd->htf', value_heads.astype(jnp.float32), merged_state, precision=highest) + merged_total[:, None, :]
        value_total = grad_vblk + jnp.einsum('htf,hfd->htd', key_feat.astype(jnp.float32), merged_state, precision=highest)
        key_grad = feature_back(kfeat_total, key_one, key_two, proj_wide)
        return key_grad.transpose(1, 0, 2).astype(jnp.bfloat16), value_total.transpose(1, 0, 2).astype(jnp.bfloat16)

    dk_blocks, dv_blocks = lax.map(backward_block, (key_blocks, value_blocks, grad_kfeat, grad_value, suffix[0], suffix[1]))
    return (dq_blocks.reshape(TOKENS, GROUP, KVH, HD), dk_blocks.reshape(TOKENS, KVH, HD), dv_blocks.reshape(TOKENS, KVH, HD))
```

```python
import jax
import jax.numpy as jnp
from jax import lax
from jax.experimental import pallas as pl
from jax.experimental.pallas import tpu as pltpu
from jax.sharding import PartitionSpec as P

f32 = jnp.float32
bf16 = jnp.bfloat16
GRANT = 56 * 1024 * 1024


def dot(first, second, dims):
    return lax.dot_general(first, second, (dims, ((), ())), preferred_element_type=f32)


def nn(first, second):
    return dot(first, second, ((1,), (0,)))


def nt(first, second):
    return dot(first, second, ((1,), (1,)))


def pair_count(width):
    return width * width // 2 + width // 2


def sketches(tokens, proj, width):
    both = dot(proj, tokens, ((0,), (1,))) * tokens.shape[-1] ** (-0.5)
    return both[:width], both[width:]


def pair_features(s):
    width = s.shape[0]
    half = width // 2
    scaled = s * (1.0 / width)
    parts = [(scaled * s).astype(bf16)]
    for d in range(1, half):
        parts.append((scaled * pltpu.roll(s, width - d, 0)).astype(bf16))
    parts.append((scaled[:half] * s[half:]).astype(bf16))
    return jnp.concatenate(parts, axis=0)


def pair_back(c, s):
    width = s.shape[0]
    half = width // 2
    acc = c[:width] * s
    for d in range(1, half):
        one = c[d * width : (d + 1) * width]
        acc = acc + one * pltpu.roll(s, width - d, 0) + pltpu.roll(one * s, d, 0)
    last = c[half * width :]
    acc = acc + jnp.concatenate([last * s[half:], last * s[:half]], axis=0)
    return acc * (2.0 / width)


def doubled(rows, width, axis):
    place = lax.broadcasted_iota(jnp.int32, rows.shape, axis)
    return jnp.where(place < width, rows, rows * 2.0)


def split(a):
    high = a.astype(bf16)
    return high, (a - high.astype(f32)).astype(bf16)


def finish(ds, one, two, proj, scale):
    high, low = split(jnp.concatenate([ds * two, ds * one], axis=0))
    both = jnp.concatenate([proj, proj], axis=1)
    return dot(jnp.concatenate([high, low], axis=0), both, ((0,), (1,))) * scale


def pack_totals(column, lanes):
    count = column.shape[0]
    row = column.T[:1]
    rows = []
    for start in range(0, count, lanes):
        piece = row[:, start : start + lanes]
        if piece.shape[1] < lanes:
            piece = jnp.concatenate(
                [piece, jnp.zeros((1, lanes - piece.shape[1]), f32)], axis=1
            )
        rows.append(piece)
    rows.append(jnp.zeros((16 - len(rows), lanes), f32))
    return jnp.concatenate(rows, axis=0)


def unpack_totals(packed, count):
    lanes = packed.shape[1]
    parts = [packed[k : k + 1] for k in range(-(-count // lanes))]
    return jnp.concatenate(parts, axis=1)[:, :count]


def ones_beside(v):
    lane = lax.broadcasted_iota(jnp.int32, v.shape, 1)
    return jnp.concatenate([v, jnp.where(lane == 0, 1.0, 0.0).astype(bf16)], axis=1)


def state_with_totals(wide, lanes):
    return jnp.concatenate([wide[:, :lanes], pack_totals(wide[:, lanes:], lanes)], axis=0)


def first_kernel(q_ref, k_ref, v_ref, proj_ref, s_ref, state_ref):
    proj = proj_ref[...]
    width = proj.shape[1] // 2

    @pl.loop(0, k_ref.shape[0])
    def _(h):
        one, two = sketches(k_ref[h], proj, width)
        feat = pair_features((one * two).astype(bf16).astype(f32))
        v = v_ref[h]
        wide = nn(feat, ones_beside(v))
        state_ref[h] = state_with_totals(wide, v.shape[1]).astype(bf16)

    @pl.loop(0, q_ref.shape[0])
    def _(m):
        @pl.loop(0, q_ref.shape[1])
        def _(h):
            one, two = sketches(q_ref[m, h], proj, width)
            s_ref[m, h] = (one * two).astype(bf16)


def main_kernel(
    sq_ref, k_ref, v_ref, g_ref, proj_ref, state_ref, dsq_ref, dsk_ref, dv_ref, out_ref
):
    proj = proj_ref[...]
    width = proj.shape[1] // 2
    pairs = pair_count(width)
    members = sq_ref.shape[0]
    tokens, lanes = v_ref.shape[1:]
    one, two = sketches(k_ref[0], proj, width)
    skt = (one * two).astype(bf16)
    sk = (one * two).T.astype(bf16)
    v = v_ref[0]
    sqt = jnp.concatenate([sq_ref[m, 0] for m in range(members)], axis=1)
    sq = sqt.astype(f32)
    gout = jnp.concatenate([g_ref[m, 0].astype(f32).T for m in range(members)], axis=1)
    feat = pair_features(sq)
    state = state_ref[0][:pairs]
    totals = unpack_totals(state_ref[0][pairs:], pairs)

    inside = nn(sk, sqt)
    row = lax.broadcasted_iota(jnp.int32, inside.shape, 0)
    column = lax.rem(lax.broadcasted_iota(jnp.int32, inside.shape, 1), tokens)
    inside = jnp.where(row <= column, inside, 0.0)
    weights = (inside * inside * (1.0 / width**2)).astype(bf16)
    left = jnp.concatenate([v.astype(f32).T, jnp.ones((8, tokens), f32)], axis=0).astype(bf16)
    total_high = totals.astype(bf16).astype(f32)
    total_rows = jnp.concatenate(
        [total_high, totals - total_high, jnp.zeros((6, pairs), f32)], axis=0
    )
    state_rows = doubled(jnp.concatenate([state.T, total_rows], axis=0), width, 1).astype(bf16)
    over = nn(left, weights) + nn(state_rows, feat)
    low_total = nn(state_rows[lanes:], feat)[1:2]
    scale = 1.0 / (1.0 + over[lanes : lanes + 1] + low_total)
    rows = gout * scale
    correction = -jnp.sum(rows * over[:lanes], axis=0, keepdims=True) * scale
    low = rows.astype(bf16)
    dscores = nn(v, low) + correction
    edge = (dscores * inside * (2.0 / width**2)).astype(bf16)
    dsk_ref[0] = nt(edge, sqt)
    dv_ref[0] = nt(weights, low)

    corr_high = correction.astype(bf16).astype(f32)
    corr_rows = jnp.concatenate(
        [corr_high, correction - corr_high, jnp.zeros((lanes - 2, sq.shape[1]), f32)], axis=0
    ).astype(bf16)
    spread = jnp.concatenate([low, corr_rows], axis=0)
    total_columns = jnp.concatenate(
        [totals, totals, jnp.zeros((lanes - 2, pairs), f32)], axis=0
    ).T
    cotangent = nn(jnp.concatenate([state, total_columns], axis=1).astype(bf16), spread)
    dsq = nn(skt, edge) + pair_back(cotangent, sq)
    for m in range(members):
        dsq_ref[m, 0] = dsq[:, m * tokens : (m + 1) * tokens].astype(bf16)

    wide = nt(feat, spread)
    both = wide[:, lanes:] + pltpu.roll(wide[:, lanes:], lanes - 1, 1)
    out_ref[0] = state_with_totals(jnp.concatenate([wide[:, :lanes], both], axis=1), lanes).astype(
        bf16
    )


def last_kernel(
    q_ref, ds_ref, k_ref, v_ref, proj_ref, state_ref, dsk_ref, dv_ref, dq_ref, dk_ref, dvo_ref
):
    proj = proj_ref[...]
    width = proj.shape[1] // 2
    pairs = pair_count(width)
    inverse = k_ref.shape[-1] ** (-0.5)

    @pl.loop(0, k_ref.shape[0])
    def _(h):
        one, two = sketches(k_ref[h], proj, width)
        s = (one * two).astype(bf16).astype(f32)
        feat = pair_features(s)
        v = v_ref[h]
        lanes = v.shape[1]
        state = state_ref[h][:pairs]
        totals = unpack_totals(state_ref[h][pairs:], pairs)
        total_columns = jnp.concatenate([totals, jnp.zeros((lanes - 1, pairs), f32)], axis=0).T
        cotangent = nt(
            jnp.concatenate([state, total_columns], axis=1).astype(bf16), ones_beside(v)
        )
        ds = dsk_ref[h].T + pair_back(cotangent, s)
        dk_ref[h] = finish(ds, one, two, proj, inverse).astype(bf16)
        state_rows = doubled(state.T, width, 1).astype(bf16)
        dvo_ref[h] = (dv_ref[h] + nn(state_rows, feat).T).astype(bf16)

    @pl.loop(0, q_ref.shape[0])
    def _(m):
        @pl.loop(0, q_ref.shape[1])
        def _(h):
            one, two = sketches(q_ref[m, h], proj, width)
            ds = ds_ref[m, h].astype(f32)
            dq_ref[m, h] = finish(ds, one, two, proj, inverse).astype(bf16)


def call(kernel, outs, args, **more):
    return pl.pallas_call(
        kernel,
        out_shape=outs,
        compiler_params=pltpu.CompilerParams(vmem_limit_bytes=GRANT),
        **more,
    )(*args)


def body(queries, keys, values, dout, signs):
    proj = jnp.concatenate([2 * signs[0] - 1, 2 * signs[1] - 1], axis=1).astype(bf16)
    width = signs.shape[-1]
    pairs = pair_count(width)
    rows = pairs + 16
    heads_all = keys.shape[1]
    owned = heads_all // lax.axis_size("head")
    offset = lax.axis_index("head") * owned
    k = lax.dynamic_slice_in_dim(keys, offset, owned, 1).transpose(1, 0, 2)
    v = lax.dynamic_slice_in_dim(values, offset, owned, 1).transpose(1, 0, 2)
    q = queries.transpose(1, 2, 0, 3)
    g = dout.transpose(1, 2, 0, 3)
    mine, _, tokens, hd = q.shape
    members = mine * lax.axis_size("head")
    shape = jax.ShapeDtypeStruct
    sq, block_state = call(
        first_kernel,
        (shape((mine, heads_all, width, tokens), bf16), shape((owned, rows, hd), bf16)),
        (q, k, v, proj),
    )
    sq = lax.all_to_all(sq, "head", split_axis=1, concat_axis=0, tiled=True)
    g = lax.all_to_all(g, "head", split_axis=1, concat_axis=0, tiled=True)
    count = lax.axis_size("ctx")
    place = lax.axis_index("ctx")
    source = lax.broadcasted_iota(jnp.int32, (count, 1, 1, 1), 0)

    def scan(part, keep):
        gathered = lax.all_gather(part, "ctx")
        return jnp.sum(jnp.where(keep, gathered.astype(f32), 0.0), 0)

    state = scan(block_state, source < place)
    by_member = lambda h: (0, h, 0, 0)
    by_head = lambda h: (h, 0, 0)
    dsq, dsk, dv, part = call(
        main_kernel,
        (
            shape((members, owned, width, tokens), bf16),
            shape((owned, tokens, width), f32),
            shape((owned, tokens, hd), f32),
            shape((owned, rows, hd), bf16),
        ),
        (sq, k, v, g, proj, state),
        grid=(owned,),
        in_specs=[
            pl.BlockSpec((members, 1, width, tokens), by_member),
            pl.BlockSpec((1, tokens, hd), by_head),
            pl.BlockSpec((1, tokens, hd), by_head),
            pl.BlockSpec((members, 1, tokens, hd), by_member),
            pl.BlockSpec((hd, 2 * width), lambda h: (0, 0)),
            pl.BlockSpec((1, rows, hd), by_head),
        ],
        out_specs=(
            pl.BlockSpec((members, 1, width, tokens), by_member),
            pl.BlockSpec((1, tokens, width), by_head),
            pl.BlockSpec((1, tokens, hd), by_head),
            pl.BlockSpec((1, rows, hd), by_head),
        ),
    )
    dsq = lax.all_to_all(dsq, "head", split_axis=0, concat_axis=1, tiled=True)
    later = scan(part, source > place)
    dq, dk, dv = call(
        last_kernel,
        (
            shape((mine, heads_all, tokens, hd), bf16),
            shape((owned, tokens, hd), bf16),
            shape((owned, tokens, hd), bf16),
        ),
        (q, dsq, k, v, proj, later, dsk, dv),
    )
    return dq.transpose(2, 0, 1, 3), dk.transpose(1, 0, 2), dv.transpose(1, 0, 2)


def solution(mesh):
    in_specs = (
        P("ctx", "head", None, None),
        P("ctx", None, None),
        P("ctx", None, None),
        P("ctx", "head", None, None),
        P(),
    )
    out_specs = (P("ctx", "head", None, None), P("ctx", "head", None), P("ctx", "head", None))
    return jax.shard_map(body, mesh=mesh, in_specs=in_specs, out_specs=out_specs, check_vma=False)
```

```python
import functools

import jax
import jax.numpy as jnp
from jax import lax
from jax.experimental import pallas as pl
from jax.experimental.pallas import tpu as pltpu
from jax.sharding import PartitionSpec as P

f32 = jnp.float32
bf16 = jnp.bfloat16
GRANT = 56 * 1024 * 1024


def dot(first, second, dims):
    return lax.dot_general(first, second, (dims, ((), ())), preferred_element_type=f32)


def nn(first, second):
    return dot(first, second, ((1,), (0,)))


def nt(first, second):
    return dot(first, second, ((1,), (1,)))


def pair_count(width):
    return width * width // 2 + width // 2


def sketches(tokens, proj, width):
    both = dot(proj, tokens, ((0,), (1,))) * tokens.shape[-1] ** (-0.5)
    return both[:width], both[width:]


def pair_features(s):
    width = s.shape[0]
    half = width // 2
    scaled = s * (1.0 / width)
    parts = [(scaled * s).astype(bf16)]
    for d in range(1, half):
        parts.append((scaled * pltpu.roll(s, width - d, 0)).astype(bf16))
    parts.append((scaled[:half] * s[half:]).astype(bf16))
    return jnp.concatenate(parts, axis=0)


def pair_back(c, s):
    width = s.shape[0]
    half = width // 2
    acc = c[:width] * s
    for d in range(1, half):
        one = c[d * width : (d + 1) * width]
        acc = acc + one * pltpu.roll(s, width - d, 0) + pltpu.roll(one * s, d, 0)
    last = c[half * width :]
    acc = acc + jnp.concatenate([last * s[half:], last * s[:half]], axis=0)
    return acc * (2.0 / width)


def doubled(rows, width, axis):
    place = lax.broadcasted_iota(jnp.int32, rows.shape, axis)
    return jnp.where(place < width, rows, rows * 2.0)


def split(a):
    high = a.astype(bf16)
    return high, (a - high.astype(f32)).astype(bf16)


def finish(ds, one, two, proj, scale):
    high, low = split(jnp.concatenate([ds * two, ds * one], axis=0))
    both = jnp.concatenate([proj, proj], axis=1)
    return dot(jnp.concatenate([high, low], axis=0), both, ((0,), (1,))) * scale


def pack_totals(column, lanes):
    count = column.shape[0]
    row = column.T[:1]
    rows = []
    for start in range(0, count, lanes):
        piece = row[:, start : start + lanes]
        if piece.shape[1] < lanes:
            piece = jnp.concatenate(
                [piece, jnp.zeros((1, lanes - piece.shape[1]), f32)], axis=1
            )
        rows.append(piece)
    rows.append(jnp.zeros((16 - len(rows), lanes), f32))
    return jnp.concatenate(rows, axis=0)


def unpack_totals(packed, count):
    lanes = packed.shape[1]
    parts = [packed[k : k + 1] for k in range(-(-count // lanes))]
    return jnp.concatenate(parts, axis=1)[:, :count]


def ones_beside(v):
    lane = lax.broadcasted_iota(jnp.int32, v.shape, 1)
    return jnp.concatenate([v, jnp.where(lane == 0, 1.0, 0.0).astype(bf16)], axis=1)


def state_with_totals(wide, lanes):
    return jnp.concatenate([wide[:, :lanes], pack_totals(wide[:, lanes:], lanes)], axis=0)


def first_kernel(q_ref, k_ref, v_ref, proj_ref, s_ref, state_ref):
    proj = proj_ref[...]
    width = proj.shape[1] // 2

    @pl.loop(0, k_ref.shape[0])
    def _(h):
        one, two = sketches(k_ref[h], proj, width)
        feat = pair_features(one * two)
        v = v_ref[h]
        wide = nn(feat, ones_beside(v))
        state_ref[h] = state_with_totals(wide, v.shape[1]).astype(bf16)

    @pl.loop(0, q_ref.shape[0])
    def _(m):
        @pl.loop(0, q_ref.shape[1])
        def _(h):
            one, two = sketches(q_ref[m, h], proj, width)
            s_ref[m, h] = jnp.concatenate(split(one * two), axis=0)


def main_kernel(
    sq_ref, k_ref, v_ref, g_ref, proj_ref, state_ref, dsq_ref, dsk_ref, dv_ref, out_ref
):
    proj = proj_ref[...]
    width = proj.shape[1] // 2
    pairs = pair_count(width)
    members = sq_ref.shape[0]
    tokens, lanes = v_ref.shape[1:]
    one, two = sketches(k_ref[0], proj, width)
    skt = jnp.concatenate(split(one * two), axis=0)
    sk_high, sk_low = split((one * two).T)
    v = v_ref[0]
    sqt = jnp.concatenate([sq_ref[m, 0] for m in range(members)], axis=1)
    sq = sqt[:width].astype(f32) + sqt[width:].astype(f32)
    gout = jnp.concatenate([g_ref[m, 0].astype(f32).T for m in range(members)], axis=1)
    feat = pair_features(sq)
    held = state_ref[0].astype(f32)
    state = held[:pairs]
    totals = unpack_totals(held[pairs:], pairs)

    inside = nn(
        jnp.concatenate([sk_high, sk_high, sk_low], axis=1),
        jnp.concatenate([sqt, sqt[:width]], axis=0),
    )
    row = lax.broadcasted_iota(jnp.int32, inside.shape, 0)
    column = lax.rem(lax.broadcasted_iota(jnp.int32, inside.shape, 1), tokens)
    inside = jnp.where(row <= column, inside, 0.0)
    weights = (inside * inside * (1.0 / width**2)).astype(bf16)
    left = jnp.concatenate([v.astype(f32).T, jnp.ones((8, tokens), f32)], axis=0).astype(bf16)
    total_high = totals.astype(bf16).astype(f32)
    total_rows = jnp.concatenate(
        [total_high, totals - total_high, jnp.zeros((6, pairs), f32)], axis=0
    )
    state_rows = doubled(jnp.concatenate([state.T, total_rows], axis=0), width, 1).astype(bf16)
    over = nn(left, weights) + nn(state_rows, feat)
    low_total = nn(state_rows[lanes:], feat)[1:2]
    scale = 1.0 / (1.0 + over[lanes : lanes + 1] + low_total)
    rows = gout * scale
    correction = -jnp.sum(rows * over[:lanes], axis=0, keepdims=True) * scale
    low = rows.astype(bf16)
    dscores = nn(v, low) + correction
    edge = (dscores * inside * (2.0 / width**2)).astype(bf16)
    dsk_both = nt(edge, sqt)
    dsk_ref[0] = dsk_both[:, :width] + dsk_both[:, width:]
    dv_ref[0] = nt(weights, low)

    corr_high = correction.astype(bf16).astype(f32)
    corr_rows = jnp.concatenate(
        [corr_high, correction - corr_high, jnp.zeros((lanes - 2, sq.shape[1]), f32)], axis=0
    ).astype(bf16)
    spread = jnp.concatenate([low, corr_rows], axis=0)
    total_columns = jnp.concatenate(
        [totals, totals, jnp.zeros((lanes - 2, pairs), f32)], axis=0
    ).T
    cotangent = nn(jnp.concatenate([state, total_columns], axis=1).astype(bf16), spread)
    dsq_both = nn(skt, edge)
    dsq = dsq_both[:width] + dsq_both[width:] + pair_back(cotangent, sq)
    for m in range(members):
        dsq_ref[m, 0] = dsq[:, m * tokens : (m + 1) * tokens].astype(bf16)

    wide = nt(feat, spread)
    both = wide[:, lanes:] + pltpu.roll(wide[:, lanes:], lanes - 1, 1)
    out_ref[0] = state_with_totals(jnp.concatenate([wide[:, :lanes], both], axis=1), lanes).astype(
        bf16
    )


def last_kernel(
    q_ref, ds_ref, k_ref, v_ref, proj_ref, state_ref, dsk_ref, dv_ref, dq_ref, dk_ref, dvo_ref
):
    proj = proj_ref[...]
    width = proj.shape[1] // 2
    pairs = pair_count(width)
    inverse = k_ref.shape[-1] ** (-0.5)

    @pl.loop(0, k_ref.shape[0])
    def _(h):
        one, two = sketches(k_ref[h], proj, width)
        s = one * two
        feat = pair_features(s)
        v = v_ref[h]
        lanes = v.shape[1]
        held = state_ref[h].astype(f32)
        state = held[:pairs]
        totals = unpack_totals(held[pairs:], pairs)
        total_columns = jnp.concatenate([totals, jnp.zeros((lanes - 1, pairs), f32)], axis=0).T
        cotangent = nt(
            jnp.concatenate([state, total_columns], axis=1).astype(bf16), ones_beside(v)
        )
        ds = dsk_ref[h].T + pair_back(cotangent, s)
        dk_ref[h] = finish(ds, one, two, proj, inverse).astype(bf16)
        state_rows = doubled(state.T, width, 1).astype(bf16)
        dvo_ref[h] = (dv_ref[h] + nn(state_rows, feat).T).astype(bf16)

    @pl.loop(0, q_ref.shape[0])
    def _(m):
        @pl.loop(0, q_ref.shape[1])
        def _(h):
            one, two = sketches(q_ref[m, h], proj, width)
            ds = ds_ref[m, h].astype(f32)
            dq_ref[m, h] = finish(ds, one, two, proj, inverse).astype(bf16)


def call(kernel, outs, args, **more):
    return pl.pallas_call(
        kernel,
        out_shape=outs,
        compiler_params=pltpu.CompilerParams(vmem_limit_bytes=GRANT),
        **more,
    )(*args)


TEAM = 4


def scan_kernel(reverse, swaps, spread, *refs):
    part = refs[0]
    sources = refs[1 : 1 + swaps]
    out = refs[1 + swaps]
    targets = refs[2 + swaps : 2 + 2 * swaps]
    (near, far, total, result, send1, recv1, send2, recv2, send3, recv3) = refs[
        2 + 2 * swaps : 12 + 2 * swaps
    ]
    send_y, recv_y, local = refs[12 + 2 * swaps :]
    blocks = lax.axis_size("ctx")
    sides = lax.axis_size("head")
    groups = blocks // TEAM
    place = lax.axis_index("ctx")
    side = lax.axis_index("head")
    rank = lax.rem(place, TEAM)
    group = place // TEAM
    step = -1 if reverse else 1
    chunks = part.shape[1]

    barrier = pltpu.get_barrier_semaphore()

    def greet(target):
        pl.semaphore_signal(
            barrier, inc=1, device_id=target, device_id_type=pl.DeviceIdType.MESH
        )

    for k in range(1, TEAM):
        greet({"ctx": group * TEAM + lax.rem(rank + k, TEAM)})
    for k in range(1, groups):
        greet({"ctx": lax.rem(group + k, groups) * TEAM + rank})
    for k in range(1, sides):
        greet({"head": lax.rem(side + k, sides)})
    pl.semaphore_wait(barrier, TEAM - 1 + groups - 1 + sides - 1)

    def remote(source, target, send, recv, device):
        return pltpu.make_async_remote_copy(
            src_ref=source,
            dst_ref=target,
            send_sem=send,
            recv_sem=recv,
            device_id=device,
            device_id_type=pl.DeviceIdType.MESH,
        )

    def member(p):
        return {"ctx": group * TEAM + p}

    def collect(p, c, slot):
        return remote(
            part.at[p, c], near.at[slot, c], send1.at[p, c], recv1.at[slot, c], member(p)
        )

    def across(k, c):
        return remote(
            total.at[c],
            far.at[k - 1, c],
            send2.at[k - 1, c],
            recv2.at[k - 1, c],
            {"ctx": (group + step * k) * TEAM + rank},
        )

    def hand(p, c, slot):
        return remote(
            result.at[p, c], out.at[slot, c], send3.at[p, c], recv3.at[slot, c], member(p)
        )

    def ahead(k):
        return group - k >= 0 if reverse else group + k < groups

    def behind(k):
        return group + k < groups if reverse else group - k >= 0

    def swap(n, k):
        source, target = sources[n], targets[n]
        to = lax.rem(side + k, sides)
        return remote(
            view(source, to), view_to(target, side), send_y.at[n, k - 1], recv_y.at[n, k - 1],
            {"head": to},
        )

    def view(source, to):
        if spread:
            count = source.shape[1] // sides
            return source.at[:, pl.ds(to * count, count)]
        count = source.shape[0] // sides
        return source.at[pl.ds(to * count, count)]

    def view_to(target, at):
        if spread:
            count = target.shape[0] // sides
            return target.at[pl.ds(at * count, count)]
        count = target.shape[1] // sides
        return target.at[:, pl.ds(at * count, count)]

    def keep(n):
        return pltpu.make_async_copy(view(sources[n], side), view_to(targets[n], side), local.at[n])

    for c in range(chunks):
        for p in range(TEAM):

            @pl.when(p != rank)
            def _():
                collect(p, c, rank).start()

    for n in range(swaps):
        for k in range(1, sides):
            swap(n, k).start()
        keep(n).start()

    for c in range(chunks):
        near[rank, c] = part[rank, c]
        for p in range(TEAM):

            @pl.when(p != rank)
            def _():
                collect(p, c, p).wait_recv()

        total[c] = sum(near[p, c].astype(f32) for p in range(TEAM)).astype(bf16)
        for k in range(1, groups):

            @pl.when(ahead(k))
            def _():
                across(k, c).start()

    zeros = jnp.zeros(part.shape[2:], f32)
    for c in range(chunks):
        running = zeros
        for k in range(1, groups):

            @pl.when(behind(k))
            def _():
                across(k, c).wait_recv()

            @pl.when(jnp.logical_not(behind(k)))
            def _():
                far[k - 1, c] = zeros.astype(bf16)

            running = running + far[k - 1, c].astype(f32)
        for p in reversed(range(TEAM)) if reverse else range(TEAM):
            result[p, c] = running.astype(bf16)
            running = running + near[p, c].astype(f32)

            @pl.when(p != rank)
            def _():
                hand(p, c, rank).start()

        out[rank, c] = result[rank, c]

    for c in range(chunks):
        for p in range(TEAM):

            @pl.when(p != rank)
            def _():
                hand(p, c, p).wait_recv()

    for n in range(swaps):
        for k in range(1, sides):
            swap(n, k).wait_recv()
            swap(n, k).wait_send()
        keep(n).wait()
    for c in range(chunks):
        for p in range(TEAM):

            @pl.when(p != rank)
            def _():
                collect(p, c, rank).wait_send()
                hand(p, c, rank).wait_send()

        for k in range(1, groups):

            @pl.when(ahead(k))
            def _():
                across(k, c).wait_send()


def scan(part, others, reverse, spread, number):
    heads, rows, lanes = part.shape
    piece = heads * rows // TEAM
    chunks = 2 if piece % 32 == 0 else 1
    shape = (TEAM, chunks, piece // chunks, lanes)
    sides = lax.axis_size("head")
    groups = lax.axis_size("ctx") // TEAM
    swaps = len(others)
    whole = pl.BlockSpec(memory_space=pltpu.VMEM)
    apart = pl.BlockSpec(memory_space=pl.ANY)
    sems = pltpu.SemaphoreType.DMA

    def moved(a):
        one, two = a.shape[:2]
        lead = (one * sides, two // sides) if spread else (one // sides, two * sides)
        return jax.ShapeDtypeStruct(lead + a.shape[2:], a.dtype)

    results = pl.pallas_call(
        functools.partial(scan_kernel, reverse, swaps, spread),
        out_shape=(jax.ShapeDtypeStruct(shape, bf16),) + tuple(moved(a) for a in others),
        in_specs=[whole] + [apart] * swaps,
        out_specs=(whole,) + (apart,) * swaps,
        scratch_shapes=[
            pltpu.VMEM(shape, bf16),
            pltpu.VMEM((max(groups - 1, 1),) + shape[1:], bf16),
            pltpu.VMEM(shape[1:], bf16),
            pltpu.VMEM(shape, bf16),
            sems((TEAM, chunks)),
            sems((TEAM, chunks)),
            sems((max(groups - 1, 1), chunks)),
            sems((max(groups - 1, 1), chunks)),
            sems((TEAM, chunks)),
            sems((TEAM, chunks)),
            sems((swaps, max(sides - 1, 1))),
            sems((swaps, max(sides - 1, 1))),
            sems((swaps,)),
        ],
        compiler_params=pltpu.CompilerParams(
            collective_id=number, has_side_effects=True, vmem_limit_bytes=GRANT
        ),
    )(part.reshape(shape), *others)
    return (results[0].reshape(part.shape),) + tuple(results[1:])


def body(queries, keys, values, dout, signs):
    proj = jnp.concatenate([2 * signs[0] - 1, 2 * signs[1] - 1], axis=1).astype(bf16)
    width = signs.shape[-1]
    pairs = pair_count(width)
    rows = pairs + 16
    heads_all = keys.shape[1]
    owned = heads_all // lax.axis_size("head")
    offset = lax.axis_index("head") * owned
    k = lax.dynamic_slice_in_dim(keys, offset, owned, 1).transpose(1, 0, 2)
    v = lax.dynamic_slice_in_dim(values, offset, owned, 1).transpose(1, 0, 2)
    q = queries.transpose(1, 2, 0, 3)
    g = dout.transpose(1, 2, 0, 3)
    mine, _, tokens, hd = q.shape
    members = mine * lax.axis_size("head")
    shape = jax.ShapeDtypeStruct
    sq, block_state = call(
        first_kernel,
        (shape((mine, heads_all, 2 * width, tokens), bf16), shape((owned, rows, hd), bf16)),
        (q, k, v, proj),
    )
    state, sq, g = scan(block_state, (sq, g), False, True, 0)
    by_member = lambda h: (0, h, 0, 0)
    by_head = lambda h: (h, 0, 0)
    dsq, dsk, dv, part = call(
        main_kernel,
        (
            shape((members, owned, width, tokens), bf16),
            shape((owned, tokens, width), f32),
            shape((owned, tokens, hd), f32),
            shape((owned, rows, hd), bf16),
        ),
        (sq, k, v, g, proj, state),
        grid=(owned,),
        in_specs=[
            pl.BlockSpec((members, 1, 2 * width, tokens), by_member),
            pl.BlockSpec((1, tokens, hd), by_head),
            pl.BlockSpec((1, tokens, hd), by_head),
            pl.BlockSpec((members, 1, tokens, hd), by_member),
            pl.BlockSpec((hd, 2 * width), lambda h: (0, 0)),
            pl.BlockSpec((1, rows, hd), by_head),
        ],
        out_specs=(
            pl.BlockSpec((members, 1, width, tokens), by_member),
            pl.BlockSpec((1, tokens, width), by_head),
            pl.BlockSpec((1, tokens, hd), by_head),
            pl.BlockSpec((1, rows, hd), by_head),
        ),
    )
    later, dsq = scan(part, (dsq,), True, False, 1)
    dq, dk, dv = call(
        last_kernel,
        (
            shape((mine, heads_all, tokens, hd), bf16),
            shape((owned, tokens, hd), bf16),
            shape((owned, tokens, hd), bf16),
        ),
        (q, dsq, k, v, proj, later, dsk, dv),
    )
    return dq.transpose(2, 0, 1, 3), dk.transpose(1, 0, 2), dv.transpose(1, 0, 2)


def solution(mesh):
    in_specs = (
        P("ctx", "head", None, None),
        P("ctx", None, None),
        P("ctx", None, None),
        P("ctx", "head", None, None),
        P(),
    )
    out_specs = (P("ctx", "head", None, None), P("ctx", "head", None), P("ctx", "head", None))
    return jax.shard_map(body, mesh=mesh, in_specs=in_specs, out_specs=out_specs, check_vma=False)
```

```python
import jax
import jax.numpy as jnp
from jax import lax
from jax.experimental import pallas as pl
from jax.experimental.pallas import tpu as pltpu
from jax.sharding import PartitionSpec as P

f32 = jnp.float32
bf16 = jnp.bfloat16
GRANT = 56 * 1024 * 1024


def dot(first, second, dims):
    return lax.dot_general(first, second, (dims, ((), ())), preferred_element_type=f32)


def nn(first, second):
    return dot(first, second, ((1,), (0,)))


def nt(first, second):
    return dot(first, second, ((1,), (1,)))


def pair_count(width):
    return width * width // 2 + width // 2


def sketches(tokens, proj, width):
    both = dot(proj, tokens, ((0,), (1,))) * tokens.shape[-1] ** (-0.5)
    return both[:width], both[width:]


def pair_features(s):
    width = s.shape[0]
    half = width // 2
    scaled = s * (1.0 / width)
    parts = [(scaled * s).astype(bf16)]
    for d in range(1, half):
        parts.append((scaled * pltpu.roll(s, width - d, 0)).astype(bf16))
    parts.append((scaled[:half] * s[half:]).astype(bf16))
    return jnp.concatenate(parts, axis=0)


def pair_back(c, s):
    width = s.shape[0]
    half = width // 2
    acc = c[:width] * s
    for d in range(1, half):
        one = c[d * width : (d + 1) * width]
        acc = acc + one * pltpu.roll(s, width - d, 0) + pltpu.roll(one * s, d, 0)
    last = c[half * width :]
    acc = acc + jnp.concatenate([last * s[half:], last * s[:half]], axis=0)
    return acc * (2.0 / width)


def doubled(rows, width, axis):
    place = lax.broadcasted_iota(jnp.int32, rows.shape, axis)
    return jnp.where(place < width, rows, rows * 2.0)


def split(a):
    high = a.astype(bf16)
    return high, (a - high.astype(f32)).astype(bf16)


def finish(ds, one, two, proj, scale):
    high, low = split(jnp.concatenate([ds * two, ds * one], axis=0))
    both = jnp.concatenate([proj, proj], axis=1)
    return dot(jnp.concatenate([high, low], axis=0), both, ((0,), (1,))) * scale


def pack_totals(column, lanes):
    count = column.shape[0]
    row = column.T[:1]
    rows = []
    for start in range(0, count, lanes):
        piece = row[:, start : start + lanes]
        if piece.shape[1] < lanes:
            piece = jnp.concatenate(
                [piece, jnp.zeros((1, lanes - piece.shape[1]), f32)], axis=1
            )
        rows.append(piece)
    rows.append(jnp.zeros((16 - len(rows), lanes), f32))
    return jnp.concatenate(rows, axis=0)


def unpack_totals(packed, count):
    lanes = packed.shape[1]
    parts = [packed[k : k + 1] for k in range(-(-count // lanes))]
    return jnp.concatenate(parts, axis=1)[:, :count]


def ones_beside(v):
    lane = lax.broadcasted_iota(jnp.int32, v.shape, 1)
    return jnp.concatenate([v, jnp.where(lane == 0, 1.0, 0.0).astype(bf16)], axis=1)


def state_with_totals(wide, lanes):
    return jnp.concatenate([wide[:, :lanes], pack_totals(wide[:, lanes:], lanes)], axis=0)


def main_kernel(
    sq_ref, k_ref, v_ref, g_ref, proj_ref, state_ref, dsq_ref, dsk_ref, dv_ref, out_ref
):
    proj = proj_ref[...]
    width = proj.shape[1] // 2
    pairs = pair_count(width)
    members = sq_ref.shape[0]
    tokens, lanes = v_ref.shape[1:]
    one, two = sketches(k_ref[0], proj, width)
    skt = jnp.concatenate(split(one * two), axis=0)
    sk_high, sk_low = split((one * two).T)
    v = v_ref[0]
    sqt = jnp.concatenate([sq_ref[m, 0] for m in range(members)], axis=1)
    sq = sqt[:width].astype(f32) + sqt[width:].astype(f32)
    gout = jnp.concatenate([g_ref[m, 0].astype(f32).T for m in range(members)], axis=1)
    feat = pair_features(sq)
    held = state_ref[0].astype(f32)
    state = held[:pairs]
    totals = unpack_totals(held[pairs:], pairs)

    inside = nn(
        jnp.concatenate([sk_high, sk_high, sk_low], axis=1),
        jnp.concatenate([sqt, sqt[:width]], axis=0),
    )
    row = lax.broadcasted_iota(jnp.int32, inside.shape, 0)
    column = lax.rem(lax.broadcasted_iota(jnp.int32, inside.shape, 1), tokens)
    inside = jnp.where(row <= column, inside, 0.0)
    weights = (inside * inside * (1.0 / width**2)).astype(bf16)
    left = jnp.concatenate([v.astype(f32).T, jnp.ones((8, tokens), f32)], axis=0).astype(bf16)
    total_high = totals.astype(bf16).astype(f32)
    total_rows = jnp.concatenate(
        [total_high, totals - total_high, jnp.zeros((6, pairs), f32)], axis=0
    )
    state_rows = doubled(jnp.concatenate([state.T, total_rows], axis=0), width, 1).astype(bf16)
    over = nn(left, weights) + nn(state_rows, feat)
    low_total = nn(state_rows[lanes:], feat)[1:2]
    scale = 1.0 / (1.0 + over[lanes : lanes + 1] + low_total)
    rows = gout * scale
    correction = -jnp.sum(rows * over[:lanes], axis=0, keepdims=True) * scale
    low = rows.astype(bf16)
    dscores = nn(v, low) + correction
    edge = (dscores * inside * (2.0 / width**2)).astype(bf16)
    dsk_both = nt(edge, sqt)
    dsk_ref[0] = dsk_both[:, :width] + dsk_both[:, width:]
    dv_ref[0] = nt(weights, low)

    corr_high = correction.astype(bf16).astype(f32)
    corr_rows = jnp.concatenate(
        [corr_high, correction - corr_high, jnp.zeros((lanes - 2, sq.shape[1]), f32)], axis=0
    ).astype(bf16)
    spread = jnp.concatenate([low, corr_rows], axis=0)
    total_columns = jnp.concatenate(
        [totals, totals, jnp.zeros((lanes - 2, pairs), f32)], axis=0
    ).T
    cotangent = nn(jnp.concatenate([state, total_columns], axis=1).astype(bf16), spread)
    dsq_both = nn(skt, edge)
    dsq = dsq_both[:width] + dsq_both[width:] + pair_back(cotangent, sq)
    for m in range(members):
        dsq_ref[m, 0] = dsq[:, m * tokens : (m + 1) * tokens].astype(bf16)

    wide = nt(feat, spread)
    both = wide[:, lanes:] + pltpu.roll(wide[:, lanes:], lanes - 1, 1)
    out_ref[0] = state_with_totals(jnp.concatenate([wide[:, :lanes], both], axis=1), lanes).astype(
        bf16
    )


def call(kernel, outs, args, **more):
    return pl.pallas_call(
        kernel,
        out_shape=outs,
        compiler_params=pltpu.CompilerParams(vmem_limit_bytes=GRANT),
        **more,
    )(*args)


TEAM = 4


def run_scan(reverse, spread, part, sources, out, targets, scratch, ready, fill, early, late, final):
    (mate, chip, other, run_in, run_out, base_out, base_in, give) = scratch[:8]
    (mate_sems, chip_sems, run_sems, base_sems, give_sems, send_y, recv_y, local) = scratch[8:]
    swaps = len(sources)
    blocks = lax.axis_size("ctx")
    sides = lax.axis_size("head")
    groups = blocks // TEAM
    place = lax.axis_index("ctx")
    side = lax.axis_index("head")
    rank = lax.rem(place, TEAM)
    group = place // TEAM
    x = rank // 2
    core = lax.rem(rank, 2)
    chunks = part.shape[1]
    late_x = (1 - x if reverse else x).astype(f32)
    late_core = (1 - core if reverse else core).astype(f32)
    team = group * TEAM
    core_peer = {"ctx": team + 2 * x + 1 - core}
    chip_peer = {"ctx": team + 2 * (1 - x) + core}
    next_group = group - 1 if reverse else group + 1
    has_next = group > 0 if reverse else group < groups - 1
    has_last = group < groups - 1 if reverse else group > 0

    barrier = pltpu.get_barrier_semaphore()

    def greet(target):
        pl.semaphore_signal(
            barrier, inc=1, device_id=target, device_id_type=pl.DeviceIdType.MESH
        )

    greet(core_peer)
    greet(chip_peer)
    ends = 0
    if groups > 1:
        ends = 2
        greet({"ctx": lax.rem(group + 1, groups) * TEAM + rank})
        greet({"ctx": lax.rem(group + groups - 1, groups) * TEAM + rank})
    for k in range(1, sides):
        greet({"head": lax.rem(side + k, sides)})
    pl.semaphore_wait(barrier, 2 + ends + sides - 1)

    def remote(source, target, send, recv, device):
        return pltpu.make_async_remote_copy(
            src_ref=source,
            dst_ref=target,
            send_sem=send,
            recv_sem=recv,
            device_id=device,
            device_id_type=pl.DeviceIdType.MESH,
        )

    def to_mate(at, c):
        return remote(
            part.at[2 * at + 1 - core, c],
            mate.at[at, c],
            mate_sems.at[0, at, c],
            mate_sems.at[1, at, c],
            core_peer,
        )

    def to_chip(c):
        return remote(
            chip.at[c], other.at[c], chip_sems.at[0, c], chip_sems.at[1, c], chip_peer
        )

    def to_next(c):
        return remote(
            run_out.at[c],
            run_in.at[c],
            run_sems.at[0, c],
            run_sems.at[1, c],
            {"ctx": next_group * TEAM + rank},
        )

    def to_base(c):
        return remote(
            base_out.at[c], base_in.at[c], base_sems.at[0, c], base_sems.at[1, c], chip_peer
        )

    def to_give(at, c, to):
        return remote(
            give.at[at, c],
            out.at[2 * at + to, c],
            give_sems.at[0, at, c],
            give_sems.at[1, at, c],
            core_peer,
        )

    def swap(n, k):
        source, target = sources[n], targets[n]
        to = lax.rem(side + k, sides)
        return remote(
            view(source, to), view_to(target, side), send_y.at[n, k - 1], recv_y.at[n, k - 1],
            {"head": to},
        )

    def view(source, to):
        if spread:
            count = source.shape[1] // sides
            return source.at[:, pl.ds(to * count, count)]
        count = source.shape[0] // sides
        return source.at[pl.ds(to * count, count)]

    def view_to(target, at):
        if spread:
            count = target.shape[0] // sides
            return target.at[pl.ds(at * count, count)]
        count = target.shape[1] // sides
        return target.at[:, pl.ds(at * count, count)]

    def keep(n):
        return pltpu.make_async_copy(view(sources[n], side), view_to(targets[n], side), local.at[n])

    def wide(ref, *at):
        return ref[at].astype(f32)

    def deliver(at, c, base):
        mine, theirs = wide(part, 2 * at + core, c), wide(mate, at, c)
        give[at, c] = (base + mine * (1.0 - late_core)).astype(bf16)
        to_give(at, c, core).start()
        out[2 * at + core, c] = (base + theirs * late_core).astype(bf16)

    def begin(n):
        for k in range(1, sides):
            swap(n, k).start()
        keep(n).start()

    def end(n):
        for k in range(1, sides):
            swap(n, k).wait()
        keep(n).wait()

    for n in range(ready):
        begin(n)
    fill()
    for c in range(chunks):
        to_mate(1 - x, c).start()
        to_mate(x, c).start()

    for c in range(chunks):
        to_mate(1 - x, c).wait_recv()
        chip[c] = (wide(part, 2 * (1 - x) + core, c) + wide(mate, 1 - x, c)).astype(bf16)
        to_chip(c).start()

    early()
    for n in range(ready, swaps):
        begin(n)

    @pl.when(has_last)
    def _():
        late(end)

    for c in range(chunks):
        to_mate(x, c).wait_recv()
        to_chip(c).wait_recv()
        here = wide(part, rank, c) + wide(mate, x, c)
        there = wide(other, c)

        @pl.when(has_last)
        def _():
            to_next(c).wait_recv()

        @pl.when(jnp.logical_not(has_last))
        def _():
            run_in[c] = jnp.zeros_like(run_in[c])

        before = wide(run_in, c)
        run_out[c] = (before + here + there).astype(bf16)

        @pl.when(has_next)
        def _():
            to_next(c).start()

        base_out[c] = (before + here * (1.0 - late_x)).astype(bf16)
        to_base(c).start()
        deliver(x, c, before + there * late_x)

    @pl.when(jnp.logical_not(has_last))
    def _():
        late(end)

    for c in range(chunks):
        to_base(c).wait_recv()
        deliver(1 - x, c, wide(base_in, c))

    final(end)
    for c in range(chunks):
        for at in (x, 1 - x):
            to_give(at, c, 1 - core).wait_recv()
            to_give(at, c, core).wait_send()
            to_mate(at, c).wait_send()
        to_chip(c).wait_send()
        to_base(c).wait_send()

        @pl.when(has_next)
        def _():
            to_next(c).wait_send()


def piece_of(buffer, h, j, per):
    at = h * per + j
    return at // buffer.shape[1], lax.rem(at, buffer.shape[1])


def first_kernel(q_ref, k_ref, v_ref, g_ref, proj_ref, out, s_out, g_out, part, s_held, *scratch):
    proj = proj_ref[...]
    width = proj.shape[1] // 2
    owned = k_ref.shape[0]
    per = part.shape[0] * part.shape[1] // owned
    rows = part.shape[2]

    def fill():
        @pl.loop(0, owned)
        def _(h):
            one, two = sketches(k_ref[h], proj, width)
            v = v_ref[h]
            wide = nn(pair_features(one * two), ones_beside(v))
            state = state_with_totals(wide, v.shape[1]).astype(bf16)
            for j in range(per):
                part[piece_of(part, h, j, per)] = state[j * rows : (j + 1) * rows]

    def early():
        @pl.loop(0, q_ref.shape[0])
        def _(m):
            @pl.loop(0, q_ref.shape[1])
            def _(h):
                one, two = sketches(q_ref[m, h], proj, width)
                s_held[m, h] = jnp.concatenate(split(one * two), axis=0)

    run_scan(
        False, True, part, (g_ref, s_held), out, (g_out, s_out), scratch, 1, fill, early,
        lambda end: None,
        lambda end: (end(0), end(1)),
    )


def last_kernel(
    part, q_ref, ds_ref, k_ref, v_ref, proj_ref, dsk_ref, dv_ref, dq_ref, dk_ref, dvo_ref,
    state_ref, ds_all, *scratch,
):
    proj = proj_ref[...]
    width = proj.shape[1] // 2
    pairs = pair_count(width)
    owned = k_ref.shape[0]
    per = part.shape[0] * part.shape[1] // owned
    inverse = k_ref.shape[-1] ** (-0.5)
    side = lax.axis_index("head")
    mine, heads = q_ref.shape[:2]

    def query_gradient(m, h, ds):
        one, two = sketches(q_ref[m, h], proj, width)
        dq_ref[m, h] = finish(ds.astype(f32), one, two, proj, inverse).astype(bf16)

    def early():
        @pl.loop(0, mine)
        def _(m):
            @pl.loop(0, owned)
            def _(h):
                query_gradient(m, side * owned + h, ds_ref[side * mine + m, h])

    def late(end):
        end(0)

        @pl.loop(0, mine)
        def _(m):
            @pl.loop(owned, heads)
            def _(k):
                h = lax.rem(side * owned + k, heads)
                query_gradient(m, h, ds_all[m, h])

    run_scan(
        True, False, part, (ds_ref,), state_ref, (ds_all,), scratch, 1,
        lambda: None, early, late, lambda end: None,
    )

    @pl.loop(0, owned)
    def _(h):
        one, two = sketches(k_ref[h], proj, width)
        s = one * two
        feat = pair_features(s)
        v = v_ref[h]
        lanes = v.shape[1]
        held = jnp.concatenate(
            [state_ref[piece_of(part, h, j, per)] for j in range(per)], axis=0
        ).astype(f32)
        state = held[:pairs]
        totals = unpack_totals(held[pairs:], pairs)
        total_columns = jnp.concatenate([totals, jnp.zeros((lanes - 1, pairs), f32)], axis=0).T
        cotangent = nt(
            jnp.concatenate([state, total_columns], axis=1).astype(bf16), ones_beside(v)
        )
        ds = dsk_ref[h].T + pair_back(cotangent, s)
        dk_ref[h] = finish(ds, one, two, proj, inverse).astype(bf16)
        state_rows = doubled(state.T, width, 1).astype(bf16)
        dvo_ref[h] = (dv_ref[h] + nn(state_rows, feat).T).astype(bf16)


def pieces(heads, rows, lanes):
    piece = heads * rows // TEAM
    chunks = 2 if piece % 32 == 0 else 1
    return (TEAM, chunks, piece // chunks, lanes)


def scan_scratch(shape, swaps):
    sides = max(lax.axis_size("head") - 1, 1)
    chunks = shape[1]
    sems = pltpu.SemaphoreType.DMA
    one = pltpu.VMEM(shape[1:], bf16)
    two = pltpu.VMEM((2,) + shape[1:], bf16)
    return [
        two, one, one, one, one, one, one, two,
        sems((2, 2, chunks)),
        sems((2, chunks)),
        sems((2, chunks)),
        sems((2, chunks)),
        sems((2, 2, chunks)),
        sems((swaps, sides)),
        sems((swaps, sides)),
        sems((swaps,)),
    ]


def call_scan(kernel, outs, in_specs, out_specs, scratch, number, args):
    return pl.pallas_call(
        kernel,
        out_shape=outs,
        in_specs=in_specs,
        out_specs=out_specs,
        scratch_shapes=scratch,
        compiler_params=pltpu.CompilerParams(
            collective_id=number, has_side_effects=True, vmem_limit_bytes=GRANT
        ),
    )(*args)


def body(queries, keys, values, dout, signs):
    proj = jnp.concatenate([2 * signs[0] - 1, 2 * signs[1] - 1], axis=1).astype(bf16)
    width = signs.shape[-1]
    pairs = pair_count(width)
    rows = pairs + 16
    heads_all = keys.shape[1]
    owned = heads_all // lax.axis_size("head")
    offset = lax.axis_index("head") * owned
    k = lax.dynamic_slice_in_dim(keys, offset, owned, 1).transpose(1, 0, 2)
    v = lax.dynamic_slice_in_dim(values, offset, owned, 1).transpose(1, 0, 2)
    q = queries.transpose(1, 2, 0, 3)
    g = dout.transpose(1, 2, 0, 3)
    mine, _, tokens, hd = q.shape
    members = mine * lax.axis_size("head")
    shape = jax.ShapeDtypeStruct
    shape_in = pieces(owned, rows, hd)
    whole = pl.BlockSpec(memory_space=pltpu.VMEM)
    apart = pl.BlockSpec(memory_space=pl.ANY)
    state, sq, g = call_scan(
        first_kernel,
        (
            shape(shape_in, bf16),
            shape((members, owned, 2 * width, tokens), bf16),
            shape((members, owned, tokens, hd), bf16),
        ),
        [whole, whole, whole, apart, whole],
        (whole, apart, apart),
        [pltpu.VMEM(shape_in, bf16), pltpu.VMEM((mine, heads_all, 2 * width, tokens), bf16)]
        + scan_scratch(shape_in, 2),
        0,
        (q, k, v, g, proj),
    )
    state = state.reshape(owned, rows, hd)
    by_member = lambda h: (0, h, 0, 0)
    by_head = lambda h: (h, 0, 0)
    dsq, dsk, dv, part = call(
        main_kernel,
        (
            shape((members, owned, width, tokens), bf16),
            shape((owned, tokens, width), f32),
            shape((owned, tokens, hd), f32),
            shape((owned, rows, hd), bf16),
        ),
        (sq, k, v, g, proj, state),
        grid=(owned,),
        in_specs=[
            pl.BlockSpec((members, 1, 2 * width, tokens), by_member),
            pl.BlockSpec((1, tokens, hd), by_head),
            pl.BlockSpec((1, tokens, hd), by_head),
            pl.BlockSpec((members, 1, tokens, hd), by_member),
            pl.BlockSpec((hd, 2 * width), lambda h: (0, 0)),
            pl.BlockSpec((1, rows, hd), by_head),
        ],
        out_specs=(
            pl.BlockSpec((members, 1, width, tokens), by_member),
            pl.BlockSpec((1, tokens, width), by_head),
            pl.BlockSpec((1, tokens, hd), by_head),
            pl.BlockSpec((1, rows, hd), by_head),
        ),
    )
    dq, dk, dv = call_scan(
        last_kernel,
        (
            shape((mine, heads_all, tokens, hd), bf16),
            shape((owned, tokens, hd), bf16),
            shape((owned, tokens, hd), bf16),
        ),
        [whole] * 8,
        (whole,) * 3,
        [pltpu.VMEM(shape_in, bf16), pltpu.VMEM((mine, heads_all, width, tokens), bf16)]
        + scan_scratch(shape_in, 1),
        1,
        (part.reshape(shape_in), q, dsq, k, v, proj, dsk, dv),
    )
    return dq.transpose(2, 0, 1, 3), dk.transpose(1, 0, 2), dv.transpose(1, 0, 2)


def solution(mesh):
    in_specs = (
        P("ctx", "head", None, None),
        P("ctx", None, None),
        P("ctx", None, None),
        P("ctx", "head", None, None),
        P(),
    )
    out_specs = (P("ctx", "head", None, None), P("ctx", "head", None), P("ctx", "head", None))
    return jax.shard_map(body, mesh=mesh, in_specs=in_specs, out_specs=out_specs, check_vma=False)
```

```python
import jax
import jax.numpy as jnp
from jax import lax
from jax.experimental import pallas as pl
from jax.experimental.pallas import tpu as pltpu
from jax.sharding import PartitionSpec as P

f32 = jnp.float32
bf16 = jnp.bfloat16
GRANT = 56 * 1024 * 1024


def dot(first, second, dims):
    return lax.dot_general(first, second, (dims, ((), ())), preferred_element_type=f32)


def nn(first, second):
    return dot(first, second, ((1,), (0,)))


def nt(first, second):
    return dot(first, second, ((1,), (1,)))


def pair_count(width):
    return width * width // 2 + width // 2


def sketches(tokens, proj, width):
    both = dot(proj, tokens, ((0,), (1,))) * tokens.shape[-1] ** (-0.5)
    return both[:width], both[width:]


def pair_features(s):
    width = s.shape[0]
    half = width // 2
    scaled = s * (1.0 / width)
    parts = [(scaled * s).astype(bf16)]
    for d in range(1, half):
        parts.append((scaled * pltpu.roll(s, width - d, 0)).astype(bf16))
    parts.append((scaled[:half] * s[half:]).astype(bf16))
    return jnp.concatenate(parts, axis=0)


def pair_back(c, s):
    width = s.shape[0]
    half = width // 2
    acc = c[:width] * s
    for d in range(1, half):
        one = c[d * width : (d + 1) * width]
        acc = acc + one * pltpu.roll(s, width - d, 0) + pltpu.roll(one * s, d, 0)
    last = c[half * width :]
    acc = acc + jnp.concatenate([last * s[half:], last * s[:half]], axis=0)
    return acc * (2.0 / width)


def doubled(rows, width, axis):
    place = lax.broadcasted_iota(jnp.int32, rows.shape, axis)
    return jnp.where(place < width, rows, rows * 2.0)


def split(a):
    high = a.astype(bf16)
    return high, (a - high.astype(f32)).astype(bf16)


def finish(ds, one, two, proj, scale):
    high, low = split(jnp.concatenate([ds * two, ds * one], axis=0))
    both = jnp.concatenate([proj, proj], axis=1)
    return dot(jnp.concatenate([high, low], axis=0), both, ((0,), (1,))) * scale


def pack_totals(column, lanes, depth):
    count = column.shape[0]
    row = column.T[:1]
    rows = []
    for start in range(0, count, lanes):
        piece = row[:, start : start + lanes]
        if piece.shape[1] < lanes:
            piece = jnp.concatenate(
                [piece, jnp.zeros((1, lanes - piece.shape[1]), f32)], axis=1
            )
        rows.append(piece)
    rows.append(jnp.zeros((depth - len(rows), lanes), f32))
    return jnp.concatenate(rows, axis=0)


def unpack_totals(packed, count):
    lanes = packed.shape[1]
    parts = [packed[k : k + 1] for k in range(-(-count // lanes))]
    return jnp.concatenate(parts, axis=1)[:, :count]


def ones_beside(v):
    lane = lax.broadcasted_iota(jnp.int32, v.shape, 1)
    return jnp.concatenate([v, jnp.where(lane == 0, 1.0, 0.0).astype(bf16)], axis=1)


def state_with_totals(wide, lanes, rows):
    packed = pack_totals(wide[:, lanes:], lanes, rows - wide.shape[0])
    return jnp.concatenate([wide[:, :lanes], packed], axis=0)


def main_kernel(
    sq_ref, k_ref, v_ref, g_ref, proj_ref, state_ref, dsq_ref, dsk_ref, dv_ref, out_ref
):
    proj = proj_ref[...]
    width = proj.shape[1] // 2
    pairs = pair_count(width)
    members = sq_ref.shape[0]
    tokens, lanes = v_ref.shape[1:]
    one, two = sketches(k_ref[0], proj, width)
    skt = jnp.concatenate(split(one * two), axis=0)
    sk_high, sk_low = split((one * two).T)
    v = v_ref[0]
    sqt = jnp.concatenate([sq_ref[m, 0] for m in range(members)], axis=1)
    sq = sqt[:width].astype(f32) + sqt[width:].astype(f32)
    gout = jnp.concatenate([g_ref[m, 0].astype(f32).T for m in range(members)], axis=1)
    feat = pair_features(sq)
    held = state_ref[0].astype(f32)
    state = held[:pairs]
    totals = unpack_totals(held[pairs:], pairs)

    inside = nn(
        jnp.concatenate([sk_high, sk_high, sk_low], axis=1),
        jnp.concatenate([sqt, sqt[:width]], axis=0),
    )
    row = lax.broadcasted_iota(jnp.int32, inside.shape, 0)
    column = lax.rem(lax.broadcasted_iota(jnp.int32, inside.shape, 1), tokens)
    inside = jnp.where(row <= column, inside, 0.0)
    weights = (inside * inside * (1.0 / width**2)).astype(bf16)
    left = jnp.concatenate([v.astype(f32).T, jnp.ones((8, tokens), f32)], axis=0).astype(bf16)
    total_high = totals.astype(bf16).astype(f32)
    total_rows = jnp.concatenate(
        [total_high, totals - total_high, jnp.zeros((6, pairs), f32)], axis=0
    )
    state_rows = doubled(jnp.concatenate([state.T, total_rows], axis=0), width, 1).astype(bf16)
    over = nn(left, weights) + nn(state_rows, feat)
    low_total = nn(state_rows[lanes:], feat)[1:2]
    scale = 1.0 / (1.0 + over[lanes : lanes + 1] + low_total)
    rows = gout * scale
    correction = -jnp.sum(rows * over[:lanes], axis=0, keepdims=True) * scale
    low = rows.astype(bf16)
    dscores = nn(v, low) + correction
    edge = (dscores * inside * (2.0 / width**2)).astype(bf16)
    dsk_both = nt(edge, sqt)
    dsk_ref[0] = dsk_both[:, :width] + dsk_both[:, width:]
    dv_ref[0] = nt(weights, low)

    corr_high = correction.astype(bf16).astype(f32)
    corr_rows = jnp.concatenate(
        [corr_high, correction - corr_high, jnp.zeros((lanes - 2, sq.shape[1]), f32)], axis=0
    ).astype(bf16)
    spread = jnp.concatenate([low, corr_rows], axis=0)
    total_columns = jnp.concatenate(
        [totals, totals, jnp.zeros((lanes - 2, pairs), f32)], axis=0
    ).T
    cotangent = nn(jnp.concatenate([state, total_columns], axis=1).astype(bf16), spread)
    dsq_both = nn(skt, edge)
    dsq = dsq_both[:width] + dsq_both[width:] + pair_back(cotangent, sq)
    for m in range(members):
        dsq_ref[m, 0] = dsq[:, m * tokens : (m + 1) * tokens].astype(bf16)

    wide = nt(feat, spread)
    both = wide[:, lanes:] + pltpu.roll(wide[:, lanes:], lanes - 1, 1)
    kept = jnp.concatenate([wide[:, :lanes], both], axis=1)
    out_ref[0] = state_with_totals(kept, lanes, out_ref.shape[1]).astype(bf16)


def call(kernel, outs, args, **more):
    return pl.pallas_call(
        kernel,
        out_shape=outs,
        compiler_params=pltpu.CompilerParams(vmem_limit_bytes=GRANT),
        **more,
    )(*args)


TEAM = 4
CHUNK = 144


def run_scan(reverse, spread, part, sources, out, targets, scratch, ready, fill, early, late, final):
    (mate, chip, other, run_in, run_out, base_out, base_in, give) = scratch[:8]
    (mate_sems, chip_sems, run_sems, base_sems, give_sems, send_y, recv_y, local) = scratch[8:]
    swaps = len(sources)
    blocks = lax.axis_size("ctx")
    sides = lax.axis_size("head")
    groups = blocks // TEAM
    place = lax.axis_index("ctx")
    side = lax.axis_index("head")
    rank = lax.rem(place, TEAM)
    group = place // TEAM
    x = rank // 2
    core = lax.rem(rank, 2)
    chunks = part.shape[1]
    late_x = (1 - x if reverse else x).astype(f32)
    late_core = (1 - core if reverse else core).astype(f32)
    team = group * TEAM
    core_peer = {"ctx": team + 2 * x + 1 - core}
    chip_peer = {"ctx": team + 2 * (1 - x) + core}
    next_group = group - 1 if reverse else group + 1
    has_next = group > 0 if reverse else group < groups - 1
    has_last = group < groups - 1 if reverse else group > 0

    barrier = pltpu.get_barrier_semaphore()

    def greet(target):
        pl.semaphore_signal(
            barrier, inc=1, device_id=target, device_id_type=pl.DeviceIdType.MESH
        )

    greet(core_peer)
    greet(chip_peer)
    ends = 0
    if groups > 1:
        ends = 2
        greet({"ctx": lax.rem(group + 1, groups) * TEAM + rank})
        greet({"ctx": lax.rem(group + groups - 1, groups) * TEAM + rank})
    for k in range(1, sides):
        greet({"head": lax.rem(side + k, sides)})
    pl.semaphore_wait(barrier, 2 + ends + sides - 1)

    def remote(source, target, send, recv, device):
        return pltpu.make_async_remote_copy(
            src_ref=source,
            dst_ref=target,
            send_sem=send,
            recv_sem=recv,
            device_id=device,
            device_id_type=pl.DeviceIdType.MESH,
        )

    def to_mate(at, c):
        return remote(
            part.at[2 * at + 1 - core, c],
            mate.at[at, c],
            mate_sems.at[0, at, c],
            mate_sems.at[1, at, c],
            core_peer,
        )

    def to_chip(c):
        return remote(
            chip.at[c], other.at[c], chip_sems.at[0, c], chip_sems.at[1, c], chip_peer
        )

    def to_next(c):
        return remote(
            run_out.at[c],
            run_in.at[c],
            run_sems.at[0, c],
            run_sems.at[1, c],
            {"ctx": next_group * TEAM + rank},
        )

    def to_base(c):
        return remote(
            base_out.at[c], base_in.at[c], base_sems.at[0, c], base_sems.at[1, c], chip_peer
        )

    def to_give(at, c, to):
        return remote(
            give.at[at, c],
            out.at[2 * at + to, c],
            give_sems.at[0, at, c],
            give_sems.at[1, at, c],
            core_peer,
        )

    def swap(n, k):
        source, target = sources[n], targets[n]
        to = lax.rem(side + k, sides)
        return remote(
            view(source, to), view_to(target, side), send_y.at[n, k - 1], recv_y.at[n, k - 1],
            {"head": to},
        )

    def view(source, to):
        if spread:
            count = source.shape[1] // sides
            return source.at[:, pl.ds(to * count, count)]
        count = source.shape[0] // sides
        return source.at[pl.ds(to * count, count)]

    def view_to(target, at):
        if spread:
            count = target.shape[0] // sides
            return target.at[pl.ds(at * count, count)]
        count = target.shape[1] // sides
        return target.at[:, pl.ds(at * count, count)]

    def keep(n):
        return pltpu.make_async_copy(view(sources[n], side), view_to(targets[n], side), local.at[n])

    def wide(ref, *at):
        return ref[at].astype(f32)

    def deliver(at, c, base):
        mine, theirs = wide(part, 2 * at + core, c), wide(mate, at, c)
        give[at, c] = (base + mine * (1.0 - late_core)).astype(bf16)
        to_give(at, c, core).start()
        out[2 * at + core, c] = (base + theirs * late_core).astype(bf16)

    def begin(n):
        for k in range(1, sides):
            swap(n, k).start()
        keep(n).start()

    def end(n):
        for k in range(1, sides):
            swap(n, k).wait()
        keep(n).wait()

    for n in range(ready):
        begin(n)
    fill()
    for c in range(chunks):
        to_mate(1 - x, c).start()
        to_mate(x, c).start()

    for c in range(chunks):
        to_mate(1 - x, c).wait_recv()
        chip[c] = (wide(part, 2 * (1 - x) + core, c) + wide(mate, 1 - x, c)).astype(bf16)
        to_chip(c).start()

    passed = groups - 1 - group if reverse else group

    def first_part():
        early()
        for n in range(ready, swaps):
            begin(n)

    @pl.when(passed >= 1)
    def _():
        first_part()

    @pl.when(passed >= 2)
    def _():
        late(end)

    for c in range(chunks):
        to_mate(x, c).wait_recv()
        to_chip(c).wait_recv()
        here = wide(part, rank, c) + wide(mate, x, c)
        there = wide(other, c)

        @pl.when(has_last)
        def _():
            to_next(c).wait_recv()

        @pl.when(jnp.logical_not(has_last))
        def _():
            run_in[c] = jnp.zeros_like(run_in[c])

        before = wide(run_in, c)
        run_out[c] = (before + here + there).astype(bf16)

        @pl.when(has_next)
        def _():
            to_next(c).start()

        base_out[c] = (before + here * (1.0 - late_x)).astype(bf16)
        to_base(c).start()
        deliver(x, c, before + there * late_x)

    @pl.when(passed < 1)
    def _():
        first_part()

    @pl.when(passed < 2)
    def _():
        late(end)

    for c in range(chunks):
        to_base(c).wait_recv()
        deliver(1 - x, c, wide(base_in, c))

    final(end)
    for c in range(chunks):
        for at in (x, 1 - x):
            to_give(at, c, 1 - core).wait_recv()
            to_give(at, c, core).wait_send()
            to_mate(at, c).wait_send()
        to_chip(c).wait_send()
        to_base(c).wait_send()

        @pl.when(has_next)
        def _():
            to_next(c).wait_send()


def piece_of(buffer, h, j, per):
    at = h * per + j
    return at // buffer.shape[1], lax.rem(at, buffer.shape[1])


def first_kernel(q_ref, k_ref, v_ref, g_ref, proj_ref, out, s_out, g_out, part, s_held, *scratch):
    proj = proj_ref[...]
    width = proj.shape[1] // 2
    owned = k_ref.shape[0]
    per = part.shape[0] * part.shape[1] // owned
    rows = part.shape[2]

    def fill():
        @pl.loop(0, owned)
        def _(h):
            one, two = sketches(k_ref[h], proj, width)
            v = v_ref[h]
            wide = nn(pair_features(one * two), ones_beside(v))
            state = state_with_totals(wide, v.shape[1], per * rows).astype(bf16)
            for j in range(per):
                part[piece_of(part, h, j, per)] = state[j * rows : (j + 1) * rows]

    def early():
        @pl.loop(0, q_ref.shape[0])
        def _(m):
            @pl.loop(0, q_ref.shape[1])
            def _(h):
                one, two = sketches(q_ref[m, h], proj, width)
                s_held[m, h] = jnp.concatenate(split(one * two), axis=0)

    run_scan(
        False, True, part, (g_ref, s_held), out, (g_out, s_out), scratch, 1, fill, early,
        lambda end: None,
        lambda end: (end(0), end(1)),
    )


def last_kernel(
    part, q_ref, ds_ref, k_ref, v_ref, proj_ref, dsk_ref, dv_ref, dq_ref, dk_ref, dvo_ref,
    state_ref, ds_all, *scratch,
):
    proj = proj_ref[...]
    width = proj.shape[1] // 2
    pairs = pair_count(width)
    owned = k_ref.shape[0]
    per = part.shape[0] * part.shape[1] // owned
    inverse = k_ref.shape[-1] ** (-0.5)
    side = lax.axis_index("head")
    mine, heads = q_ref.shape[:2]

    def query_gradient(m, h, ds):
        one, two = sketches(q_ref[m, h], proj, width)
        dq_ref[m, h] = finish(ds.astype(f32), one, two, proj, inverse).astype(bf16)

    def early():
        @pl.loop(0, mine)
        def _(m):
            @pl.loop(0, owned)
            def _(h):
                query_gradient(m, side * owned + h, ds_ref[side * mine + m, h])

    def late(end):
        end(0)

        @pl.loop(0, mine)
        def _(m):
            @pl.loop(owned, heads)
            def _(k):
                h = lax.rem(side * owned + k, heads)
                query_gradient(m, h, ds_all[m, h])

    run_scan(
        True, False, part, (ds_ref,), state_ref, (ds_all,), scratch, 1,
        lambda: None, early, late, lambda end: None,
    )

    @pl.loop(0, owned)
    def _(h):
        one, two = sketches(k_ref[h], proj, width)
        s = one * two
        feat = pair_features(s)
        v = v_ref[h]
        lanes = v.shape[1]
        held = jnp.concatenate(
            [state_ref[piece_of(part, h, j, per)] for j in range(per)], axis=0
        ).astype(f32)
        state = held[:pairs]
        totals = unpack_totals(held[pairs:], pairs)
        total_columns = jnp.concatenate([totals, jnp.zeros((lanes - 1, pairs), f32)], axis=0).T
        cotangent = nt(
            jnp.concatenate([state, total_columns], axis=1).astype(bf16), ones_beside(v)
        )
        ds = dsk_ref[h].T + pair_back(cotangent, s)
        dk_ref[h] = finish(ds, one, two, proj, inverse).astype(bf16)
        state_rows = doubled(state.T, width, 1).astype(bf16)
        dvo_ref[h] = (dv_ref[h] + nn(state_rows, feat).T).astype(bf16)


def pieces(heads, rows, lanes):
    piece = heads * rows // TEAM
    chunks = piece // CHUNK if piece % CHUNK == 0 else 1
    return (TEAM, chunks, piece // chunks, lanes)


def scan_scratch(shape, swaps):
    sides = max(lax.axis_size("head") - 1, 1)
    chunks = shape[1]
    sems = pltpu.SemaphoreType.DMA
    one = pltpu.VMEM(shape[1:], bf16)
    two = pltpu.VMEM((2,) + shape[1:], bf16)
    return [
        two, one, one, one, one, one, one, two,
        sems((2, 2, chunks)),
        sems((2, chunks)),
        sems((2, chunks)),
        sems((2, chunks)),
        sems((2, 2, chunks)),
        sems((swaps, sides)),
        sems((swaps, sides)),
        sems((swaps,)),
    ]


def call_scan(kernel, outs, in_specs, out_specs, scratch, number, args):
    return pl.pallas_call(
        kernel,
        out_shape=outs,
        in_specs=in_specs,
        out_specs=out_specs,
        scratch_shapes=scratch,
        compiler_params=pltpu.CompilerParams(
            collective_id=number, has_side_effects=True, vmem_limit_bytes=GRANT
        ),
    )(*args)


def body(queries, keys, values, dout, signs):
    proj = jnp.concatenate([2 * signs[0] - 1, 2 * signs[1] - 1], axis=1).astype(bf16)
    width = signs.shape[-1]
    pairs = pair_count(width)
    rows = -(-(pairs + 16) // CHUNK) * CHUNK
    heads_all = keys.shape[1]
    owned = heads_all // lax.axis_size("head")
    offset = lax.axis_index("head") * owned
    k = lax.dynamic_slice_in_dim(keys, offset, owned, 1).transpose(1, 0, 2)
    v = lax.dynamic_slice_in_dim(values, offset, owned, 1).transpose(1, 0, 2)
    q = queries.transpose(1, 2, 0, 3)
    g = dout.transpose(1, 2, 0, 3)
    mine, _, tokens, hd = q.shape
    members = mine * lax.axis_size("head")
    shape = jax.ShapeDtypeStruct
    shape_in = pieces(owned, rows, hd)
    whole = pl.BlockSpec(memory_space=pltpu.VMEM)
    apart = pl.BlockSpec(memory_space=pl.ANY)
    state, sq, g = call_scan(
        first_kernel,
        (
            shape(shape_in, bf16),
            shape((members, owned, 2 * width, tokens), bf16),
            shape((members, owned, tokens, hd), bf16),
        ),
        [whole, whole, whole, apart, whole],
        (whole, apart, apart),
        [pltpu.VMEM(shape_in, bf16), pltpu.VMEM((mine, heads_all, 2 * width, tokens), bf16)]
        + scan_scratch(shape_in, 2),
        0,
        (q, k, v, g, proj),
    )
    state = state.reshape(owned, rows, hd)
    by_member = lambda h: (0, h, 0, 0)
    by_head = lambda h: (h, 0, 0)
    dsq, dsk, dv, part = call(
        main_kernel,
        (
            shape((members, owned, width, tokens), bf16),
            shape((owned, tokens, width), f32),
            shape((owned, tokens, hd), f32),
            shape((owned, rows, hd), bf16),
        ),
        (sq, k, v, g, proj, state),
        grid=(owned,),
        in_specs=[
            pl.BlockSpec((members, 1, 2 * width, tokens), by_member),
            pl.BlockSpec((1, tokens, hd), by_head),
            pl.BlockSpec((1, tokens, hd), by_head),
            pl.BlockSpec((members, 1, tokens, hd), by_member),
            pl.BlockSpec((hd, 2 * width), lambda h: (0, 0)),
            pl.BlockSpec((1, rows, hd), by_head),
        ],
        out_specs=(
            pl.BlockSpec((members, 1, width, tokens), by_member),
            pl.BlockSpec((1, tokens, width), by_head),
            pl.BlockSpec((1, tokens, hd), by_head),
            pl.BlockSpec((1, rows, hd), by_head),
        ),
    )
    dq, dk, dv = call_scan(
        last_kernel,
        (
            shape((mine, heads_all, tokens, hd), bf16),
            shape((owned, tokens, hd), bf16),
            shape((owned, tokens, hd), bf16),
        ),
        [whole] * 8,
        (whole,) * 3,
        [pltpu.VMEM(shape_in, bf16), pltpu.VMEM((mine, heads_all, width, tokens), bf16)]
        + scan_scratch(shape_in, 1),
        1,
        (part.reshape(shape_in), q, dsq, k, v, proj, dsk, dv),
    )
    return dq.transpose(2, 0, 1, 3), dk.transpose(1, 0, 2), dv.transpose(1, 0, 2)


def solution(mesh):
    in_specs = (
        P("ctx", "head", None, None),
        P("ctx", None, None),
        P("ctx", None, None),
        P("ctx", "head", None, None),
        P(),
    )
    out_specs = (P("ctx", "head", None, None), P("ctx", "head", None), P("ctx", "head", None))
    return jax.shard_map(body, mesh=mesh, in_specs=in_specs, out_specs=out_specs, check_vma=False)
```

```python
import jax
import jax.numpy as jnp
from jax import lax
from jax.experimental import pallas as pl
from jax.experimental.pallas import tpu as pltpu
from jax.sharding import PartitionSpec as P

f32 = jnp.float32
bf16 = jnp.bfloat16
GRANT = 56 * 1024 * 1024


def dot(first, second, dims):
    return lax.dot_general(first, second, (dims, ((), ())), preferred_element_type=f32)


def nn(first, second):
    return dot(first, second, ((1,), (0,)))


def nt(first, second):
    return dot(first, second, ((1,), (1,)))


def pair_count(width):
    return width * width // 2 + width // 2


def projector(sign_ref):
    return (2 * sign_ref[...] - 1).astype(f32).astype(bf16)


def sketches(tokens, proj, width):
    both = nt(proj, tokens) * tokens.shape[-1] ** (-0.5)
    return both[:width], both[width:]


def pair_features(s):
    width = s.shape[0]
    half = width // 2
    scaled = s * (1.0 / width)
    parts = [(scaled * s).astype(bf16)]
    for d in range(1, half):
        parts.append((scaled * pltpu.roll(s, width - d, 0)).astype(bf16))
    parts.append((scaled[:half] * s[half:]).astype(bf16))
    return jnp.concatenate(parts, axis=0)


def pair_back(c, s):
    width = s.shape[0]
    half = width // 2
    acc = c[:width] * s
    for d in range(1, half):
        one = c[d * width : (d + 1) * width]
        acc = acc + one * pltpu.roll(s, width - d, 0) + pltpu.roll(one * s, d, 0)
    last = c[half * width :]
    acc = acc + jnp.concatenate([last * s[half:], last * s[:half]], axis=0)
    return acc * (2.0 / width)


def doubled(rows, width, axis):
    place = lax.broadcasted_iota(jnp.int32, rows.shape, axis)
    return jnp.where(place < width, rows, rows * 2.0)


def split(a):
    high = a.astype(bf16)
    return high, (a - high.astype(f32)).astype(bf16)


def finish(ds, one, two, proj, scale):
    high, low = split(jnp.concatenate([ds * two, ds * one], axis=0))
    both = jnp.concatenate([proj, proj], axis=0)
    return dot(jnp.concatenate([high, low], axis=0), both, ((0,), (0,))) * scale


def pack_totals(column, lanes, depth):
    count = column.shape[0]
    row = column.T[:1]
    rows = []
    for start in range(0, count, lanes):
        piece = row[:, start : start + lanes]
        if piece.shape[1] < lanes:
            piece = jnp.concatenate(
                [piece, jnp.zeros((1, lanes - piece.shape[1]), f32)], axis=1
            )
        rows.append(piece)
    rows.append(jnp.zeros((depth - len(rows), lanes), f32))
    return jnp.concatenate(rows, axis=0)


def unpack_totals(packed, count):
    lanes = packed.shape[1]
    parts = [packed[k : k + 1] for k in range(-(-count // lanes))]
    return jnp.concatenate(parts, axis=1)[:, :count]


def ones_beside(v):
    lane = lax.broadcasted_iota(jnp.int32, v.shape, 1)
    return jnp.concatenate([v, jnp.where(lane == 0, 1.0, 0.0).astype(bf16)], axis=1)


def state_with_totals(wide, lanes, rows):
    packed = pack_totals(wide[:, lanes:], lanes, rows - wide.shape[0])
    return jnp.concatenate([wide[:, :lanes], packed], axis=0)


def main_kernel(
    sq_ref, k_ref, v_ref, g_ref, sign_ref, state_ref, dsq_ref, dsk_ref, dv_ref, out_ref
):
    proj = projector(sign_ref)
    width = proj.shape[0] // 2
    pairs = pair_count(width)
    members = sq_ref.shape[0]
    tokens, lanes = v_ref.shape[1:]
    one, two = sketches(k_ref[0], proj, width)
    skt = jnp.concatenate(split(one * two), axis=0)
    sk_high, sk_low = split((one * two).T)
    v = v_ref[0]
    sqt = jnp.concatenate([sq_ref[m, 0] for m in range(members)], axis=1)
    sq = sqt[:width].astype(f32) + sqt[width:].astype(f32)
    gout = jnp.concatenate([g_ref[m, 0].astype(f32).T for m in range(members)], axis=1)
    feat = pair_features(sq)
    held = state_ref[0].astype(f32)
    state = held[:pairs]
    totals = unpack_totals(held[pairs:], pairs)

    inside = nn(
        jnp.concatenate([sk_high, sk_high, sk_low], axis=1),
        jnp.concatenate([sqt, sqt[:width]], axis=0),
    )
    row = lax.broadcasted_iota(jnp.int32, inside.shape, 0)
    column = lax.rem(lax.broadcasted_iota(jnp.int32, inside.shape, 1), tokens)
    inside = jnp.where(row <= column, inside, 0.0)
    weights = (inside * inside * (1.0 / width**2)).astype(bf16)
    left = jnp.concatenate([v.astype(f32).T, jnp.ones((8, tokens), f32)], axis=0).astype(bf16)
    total_high = totals.astype(bf16).astype(f32)
    total_rows = jnp.concatenate(
        [total_high, totals - total_high, jnp.zeros((6, pairs), f32)], axis=0
    )
    state_rows = doubled(jnp.concatenate([state.T, total_rows], axis=0), width, 1).astype(bf16)
    over = nn(left, weights) + nn(state_rows, feat)
    low_total = nn(state_rows[lanes:], feat)[1:2]
    scale = 1.0 / (1.0 + over[lanes : lanes + 1] + low_total)
    rows = gout * scale
    correction = -jnp.sum(rows * over[:lanes], axis=0, keepdims=True) * scale
    low = rows.astype(bf16)
    dscores = nn(v, low) + correction
    edge = (dscores * inside * (2.0 / width**2)).astype(bf16)
    dsk_both = nt(edge, sqt)
    dsk_ref[0] = dsk_both[:, :width] + dsk_both[:, width:]
    dv_ref[0] = nt(weights, low)

    corr_high = correction.astype(bf16).astype(f32)
    corr_rows = jnp.concatenate(
        [corr_high, correction - corr_high, jnp.zeros((lanes - 2, sq.shape[1]), f32)], axis=0
    ).astype(bf16)
    spread = jnp.concatenate([low, corr_rows], axis=0)
    total_columns = jnp.concatenate(
        [totals, totals, jnp.zeros((lanes - 2, pairs), f32)], axis=0
    ).T
    cotangent = nn(jnp.concatenate([state, total_columns], axis=1).astype(bf16), spread)
    dsq_both = nn(skt, edge)
    dsq = dsq_both[:width] + dsq_both[width:] + pair_back(cotangent, sq)
    for m in range(members):
        dsq_ref[m, 0] = dsq[:, m * tokens : (m + 1) * tokens].astype(bf16)

    wide = nt(feat, spread)
    both = wide[:, lanes:] + pltpu.roll(wide[:, lanes:], lanes - 1, 1)
    kept = jnp.concatenate([wide[:, :lanes], both], axis=1)
    out_ref[0] = state_with_totals(kept, lanes, out_ref.shape[1]).astype(bf16)


def call(kernel, outs, args, **more):
    return pl.pallas_call(
        kernel,
        out_shape=outs,
        compiler_params=pltpu.CompilerParams(vmem_limit_bytes=GRANT),
        **more,
    )(*args)


TEAM = 4
CHUNK = 144


def run_scan(reverse, spread, part, sources, out, targets, scratch, ready, fill, early, late, final):
    (mate, chip, other, run_in, run_out, base_out, base_in, give) = scratch[:8]
    (mate_sems, chip_sems, run_sems, base_sems, give_sems, send_y, recv_y, local) = scratch[8:]
    swaps = len(sources)
    blocks = lax.axis_size("ctx")
    sides = lax.axis_size("head")
    groups = blocks // TEAM
    place = lax.axis_index("ctx")
    side = lax.axis_index("head")
    rank = lax.rem(place, TEAM)
    group = place // TEAM
    x = rank // 2
    core = lax.rem(rank, 2)
    chunks = part.shape[1]
    late_x = (1 - x if reverse else x).astype(f32)
    late_core = (1 - core if reverse else core).astype(f32)
    team = group * TEAM
    core_peer = {"ctx": team + 2 * x + 1 - core}
    chip_peer = {"ctx": team + 2 * (1 - x) + core}
    next_group = group - 1 if reverse else group + 1
    has_next = group > 0 if reverse else group < groups - 1
    has_last = group < groups - 1 if reverse else group > 0

    barrier = pltpu.get_barrier_semaphore()

    def greet(target):
        pl.semaphore_signal(
            barrier, inc=1, device_id=target, device_id_type=pl.DeviceIdType.MESH
        )

    greet(core_peer)
    greet(chip_peer)
    ends = 0
    if groups > 1:
        ends = 2
        greet({"ctx": lax.rem(group + 1, groups) * TEAM + rank})
        greet({"ctx": lax.rem(group + groups - 1, groups) * TEAM + rank})
    for k in range(1, sides):
        greet({"head": lax.rem(side + k, sides)})
    pl.semaphore_wait(barrier, 2 + ends + sides - 1)

    def remote(source, target, send, recv, device):
        return pltpu.make_async_remote_copy(
            src_ref=source,
            dst_ref=target,
            send_sem=send,
            recv_sem=recv,
            device_id=device,
            device_id_type=pl.DeviceIdType.MESH,
        )

    def to_mate(at, c):
        return remote(
            part.at[2 * at + 1 - core, c],
            mate.at[at, c],
            mate_sems.at[0, at, c],
            mate_sems.at[1, at, c],
            core_peer,
        )

    def to_chip(c):
        return remote(
            chip.at[c], other.at[c], chip_sems.at[0, c], chip_sems.at[1, c], chip_peer
        )

    def to_next(c):
        return remote(
            run_out.at[c],
            run_in.at[c],
            run_sems.at[0, c],
            run_sems.at[1, c],
            {"ctx": next_group * TEAM + rank},
        )

    def to_base(c):
        return remote(
            base_out.at[c], base_in.at[c], base_sems.at[0, c], base_sems.at[1, c], chip_peer
        )

    def to_give(at, c, to):
        return remote(
            give.at[at, c],
            out.at[2 * at + to, c],
            give_sems.at[0, at, c],
            give_sems.at[1, at, c],
            core_peer,
        )

    def swap(n, k):
        source, target = sources[n], targets[n]
        to = lax.rem(side + k, sides)
        return remote(
            view(source, to), view_to(target, side), send_y.at[n, k - 1], recv_y.at[n, k - 1],
            {"head": to},
        )

    def view(source, to):
        if spread:
            count = source.shape[1] // sides
            return source.at[:, pl.ds(to * count, count)]
        count = source.shape[0] // sides
        return source.at[pl.ds(to * count, count)]

    def view_to(target, at):
        if spread:
            count = target.shape[0] // sides
            return target.at[pl.ds(at * count, count)]
        count = target.shape[1] // sides
        return target.at[:, pl.ds(at * count, count)]

    def keep(n):
        return pltpu.make_async_copy(view(sources[n], side), view_to(targets[n], side), local.at[n])

    def wide(ref, *at):
        return ref[at].astype(f32)

    def deliver(at, c, base):
        mine, theirs = wide(part, 2 * at + core, c), wide(mate, at, c)
        give[at, c] = (base + mine * (1.0 - late_core)).astype(bf16)
        to_give(at, c, core).start()
        out[2 * at + core, c] = (base + theirs * late_core).astype(bf16)

    def begin(n):
        for k in range(1, sides):
            swap(n, k).start()
        keep(n).start()

    def end(n):
        for k in range(1, sides):
            swap(n, k).wait()
        keep(n).wait()

    for n in range(ready):
        begin(n)
    fill()
    for c in range(chunks):
        to_mate(1 - x, c).start()
        to_mate(x, c).start()

    for c in range(chunks):
        to_mate(1 - x, c).wait_recv()
        chip[c] = (wide(part, 2 * (1 - x) + core, c) + wide(mate, 1 - x, c)).astype(bf16)
        to_chip(c).start()

    passed = groups - 1 - group if reverse else group

    def first_part():
        early()
        for n in range(ready, swaps):
            begin(n)

    @pl.when(passed >= 1)
    def _():
        first_part()

    @pl.when(passed >= 2)
    def _():
        late(end)

    for c in range(chunks):
        to_mate(x, c).wait_recv()
        to_chip(c).wait_recv()
        here = wide(part, rank, c) + wide(mate, x, c)
        there = wide(other, c)

        @pl.when(has_last)
        def _():
            to_next(c).wait_recv()

        @pl.when(jnp.logical_not(has_last))
        def _():
            run_in[c] = jnp.zeros_like(run_in[c])

        before = wide(run_in, c)
        run_out[c] = (before + here + there).astype(bf16)

        @pl.when(has_next)
        def _():
            to_next(c).start()

        base_out[c] = (before + here * (1.0 - late_x)).astype(bf16)
        to_base(c).start()
        deliver(x, c, before + there * late_x)

    @pl.when(passed < 1)
    def _():
        first_part()

    @pl.when(passed < 2)
    def _():
        late(end)

    for c in range(chunks):
        to_base(c).wait_recv()
        deliver(1 - x, c, wide(base_in, c))

    final(end)
    for c in range(chunks):
        for at in (x, 1 - x):
            to_give(at, c, 1 - core).wait_recv()
            to_give(at, c, core).wait_send()
            to_mate(at, c).wait_send()
        to_chip(c).wait_send()
        to_base(c).wait_send()

        @pl.when(has_next)
        def _():
            to_next(c).wait_send()


def piece_of(buffer, h, j, per):
    at = h * per + j
    return at // buffer.shape[1], lax.rem(at, buffer.shape[1])


def first_kernel(q_ref, k_ref, v_ref, g_ref, sign_ref, out, s_out, g_out, part, s_held, *scratch):
    proj = projector(sign_ref)
    width = proj.shape[0] // 2
    owned = k_ref.shape[0]
    per = part.shape[0] * part.shape[1] // owned
    rows = part.shape[2]

    def fill():
        @pl.loop(0, owned)
        def _(h):
            one, two = sketches(k_ref[h], proj, width)
            v = v_ref[h]
            wide = nn(pair_features(one * two), ones_beside(v))
            state = state_with_totals(wide, v.shape[1], per * rows).astype(bf16)
            for j in range(per):
                part[piece_of(part, h, j, per)] = state[j * rows : (j + 1) * rows]

    def early():
        @pl.loop(0, q_ref.shape[0])
        def _(m):
            @pl.loop(0, q_ref.shape[1])
            def _(h):
                one, two = sketches(q_ref[m, h], proj, width)
                s_held[m, h] = jnp.concatenate(split(one * two), axis=0)

    run_scan(
        False, True, part, (g_ref, s_held), out, (g_out, s_out), scratch, 1, fill, early,
        lambda end: None,
        lambda end: (end(0), end(1)),
    )


def last_kernel(
    part, q_ref, ds_ref, k_ref, v_ref, sign_ref, dsk_ref, dv_ref, dq_ref, dk_ref, dvo_ref,
    state_ref, ds_all, *scratch,
):
    proj = projector(sign_ref)
    width = proj.shape[0] // 2
    pairs = pair_count(width)
    owned = k_ref.shape[0]
    per = part.shape[0] * part.shape[1] // owned
    inverse = k_ref.shape[-1] ** (-0.5)
    side = lax.axis_index("head")
    mine, heads = q_ref.shape[:2]

    def query_gradient(m, h, ds):
        one, two = sketches(q_ref[m, h], proj, width)
        dq_ref[m, h] = finish(ds.astype(f32), one, two, proj, inverse).astype(bf16)

    def early():
        @pl.loop(0, mine)
        def _(m):
            @pl.loop(0, owned)
            def _(h):
                query_gradient(m, side * owned + h, ds_ref[side * mine + m, h])

    def late(end):
        end(0)

        @pl.loop(0, mine)
        def _(m):
            @pl.loop(owned, heads)
            def _(k):
                h = lax.rem(side * owned + k, heads)
                query_gradient(m, h, ds_all[m, h])

    run_scan(
        True, False, part, (ds_ref,), state_ref, (ds_all,), scratch, 1,
        lambda: None, early, late, lambda end: None,
    )

    @pl.loop(0, owned)
    def _(h):
        one, two = sketches(k_ref[h], proj, width)
        s = one * two
        feat = pair_features(s)
        v = v_ref[h]
        lanes = v.shape[1]
        held = jnp.concatenate(
            [state_ref[piece_of(part, h, j, per)] for j in range(per)], axis=0
        ).astype(f32)
        state = held[:pairs]
        totals = unpack_totals(held[pairs:], pairs)
        total_columns = jnp.concatenate([totals, jnp.zeros((lanes - 1, pairs), f32)], axis=0).T
        cotangent = nt(
            jnp.concatenate([state, total_columns], axis=1).astype(bf16), ones_beside(v)
        )
        ds = dsk_ref[h].T + pair_back(cotangent, s)
        dk_ref[h] = finish(ds, one, two, proj, inverse).astype(bf16)
        state_rows = doubled(state.T, width, 1).astype(bf16)
        dvo_ref[h] = (dv_ref[h] + nn(state_rows, feat).T).astype(bf16)


def pieces(heads, rows, lanes):
    piece = heads * rows // TEAM
    chunks = piece // CHUNK if piece % CHUNK == 0 else 1
    return (TEAM, chunks, piece // chunks, lanes)


def scan_scratch(shape, swaps):
    sides = max(lax.axis_size("head") - 1, 1)
    chunks = shape[1]
    sems = pltpu.SemaphoreType.DMA
    one = pltpu.VMEM(shape[1:], bf16)
    two = pltpu.VMEM((2,) + shape[1:], bf16)
    return [
        two, one, one, one, one, one, one, two,
        sems((2, 2, chunks)),
        sems((2, chunks)),
        sems((2, chunks)),
        sems((2, chunks)),
        sems((2, 2, chunks)),
        sems((swaps, sides)),
        sems((swaps, sides)),
        sems((swaps,)),
    ]


def call_scan(kernel, outs, in_specs, out_specs, scratch, number, args):
    return pl.pallas_call(
        kernel,
        out_shape=outs,
        in_specs=in_specs,
        out_specs=out_specs,
        scratch_shapes=scratch,
        compiler_params=pltpu.CompilerParams(
            collective_id=number, has_side_effects=True, vmem_limit_bytes=GRANT
        ),
    )(*args)


def body(queries, keys, values, dout, signs):
    sign_rows = signs.transpose(0, 2, 1).reshape(-1, signs.shape[1])
    width = signs.shape[-1]
    pairs = pair_count(width)
    rows = -(-(pairs + 16) // CHUNK) * CHUNK
    heads_all = keys.shape[1]
    owned = heads_all // lax.axis_size("head")
    offset = lax.axis_index("head") * owned
    k = lax.dynamic_slice_in_dim(keys, offset, owned, 1).transpose(1, 0, 2)
    v = lax.dynamic_slice_in_dim(values, offset, owned, 1).transpose(1, 0, 2)
    q = queries.transpose(1, 2, 0, 3)
    g = dout.transpose(1, 2, 0, 3)
    mine, _, tokens, hd = q.shape
    members = mine * lax.axis_size("head")
    shape = jax.ShapeDtypeStruct
    shape_in = pieces(owned, rows, hd)
    whole = pl.BlockSpec(memory_space=pltpu.VMEM)
    apart = pl.BlockSpec(memory_space=pl.ANY)
    state, sq, g = call_scan(
        first_kernel,
        (
            shape(shape_in, bf16),
            shape((members, owned, 2 * width, tokens), bf16),
            shape((members, owned, tokens, hd), bf16),
        ),
        [whole, whole, whole, apart, whole],
        (whole, apart, apart),
        [pltpu.VMEM(shape_in, bf16), pltpu.VMEM((mine, heads_all, 2 * width, tokens), bf16)]
        + scan_scratch(shape_in, 2),
        0,
        (q, k, v, g, sign_rows),
    )
    state = state.reshape(owned, rows, hd)
    by_member = lambda h: (0, h, 0, 0)
    by_head = lambda h: (h, 0, 0)
    dsq, dsk, dv, part = call(
        main_kernel,
        (
            shape((members, owned, width, tokens), bf16),
            shape((owned, tokens, width), f32),
            shape((owned, tokens, hd), f32),
            shape((owned, rows, hd), bf16),
        ),
        (sq, k, v, g, sign_rows, state),
        grid=(owned,),
        in_specs=[
            pl.BlockSpec((members, 1, 2 * width, tokens), by_member),
            pl.BlockSpec((1, tokens, hd), by_head),
            pl.BlockSpec((1, tokens, hd), by_head),
            pl.BlockSpec((members, 1, tokens, hd), by_member),
            pl.BlockSpec((2 * width, hd), lambda h: (0, 0)),
            pl.BlockSpec((1, rows, hd), by_head),
        ],
        out_specs=(
            pl.BlockSpec((members, 1, width, tokens), by_member),
            pl.BlockSpec((1, tokens, width), by_head),
            pl.BlockSpec((1, tokens, hd), by_head),
            pl.BlockSpec((1, rows, hd), by_head),
        ),
    )
    dq, dk, dv = call_scan(
        last_kernel,
        (
            shape((mine, heads_all, tokens, hd), bf16),
            shape((owned, tokens, hd), bf16),
            shape((owned, tokens, hd), bf16),
        ),
        [whole] * 8,
        (whole,) * 3,
        [pltpu.VMEM(shape_in, bf16), pltpu.VMEM((mine, heads_all, width, tokens), bf16)]
        + scan_scratch(shape_in, 1),
        1,
        (part.reshape(shape_in), q, dsq, k, v, sign_rows, dsk, dv),
    )
    return dq.transpose(2, 0, 1, 3), dk.transpose(1, 0, 2), dv.transpose(1, 0, 2)


def solution(mesh):
    in_specs = (
        P("ctx", "head", None, None),
        P("ctx", None, None),
        P("ctx", None, None),
        P("ctx", "head", None, None),
        P(),
    )
    out_specs = (P("ctx", "head", None, None), P("ctx", "head", None), P("ctx", "head", None))
    return jax.shard_map(body, mesh=mesh, in_specs=in_specs, out_specs=out_specs, check_vma=False)
```

```python
import jax
import jax.numpy as jnp
from jax import lax
from jax.experimental import pallas as pl
from jax.experimental.pallas import tpu as pltpu
from jax.sharding import PartitionSpec as P

f32 = jnp.float32
bf16 = jnp.bfloat16
GRANT = 56 * 1024 * 1024


def dot(first, second, dims):
    return lax.dot_general(first, second, (dims, ((), ())), preferred_element_type=f32)


def nn(first, second):
    return dot(first, second, ((1,), (0,)))


def nt(first, second):
    return dot(first, second, ((1,), (1,)))


def pair_count(width):
    return width * width // 2 + width // 2


def projector(sign_ref):
    return (2 * sign_ref[...] - 1).astype(f32).astype(bf16)


def sketches(tokens, proj, width):
    both = nt(proj, tokens) * tokens.shape[-1] ** (-0.5)
    return both[:width], both[width:]


def pair_features(s):
    width = s.shape[0]
    half = width // 2
    scaled = s * (1.0 / width)
    parts = [(scaled * s).astype(bf16)]
    for d in range(1, half):
        parts.append((scaled * pltpu.roll(s, width - d, 0)).astype(bf16))
    parts.append((scaled[:half] * s[half:]).astype(bf16))
    return jnp.concatenate(parts, axis=0)


def pair_back(c, s):
    width = s.shape[0]
    half = width // 2
    acc = c[:width] * s
    for d in range(1, half):
        one = c[d * width : (d + 1) * width]
        acc = acc + one * pltpu.roll(s, width - d, 0) + pltpu.roll(one * s, d, 0)
    last = c[half * width :]
    acc = acc + jnp.concatenate([last * s[half:], last * s[:half]], axis=0)
    return acc * (2.0 / width)


def doubled(rows, width, axis):
    place = lax.broadcasted_iota(jnp.int32, rows.shape, axis)
    return jnp.where(place < width, rows, rows * 2.0)


def split(a):
    high = a.astype(bf16)
    return high, (a - high.astype(f32)).astype(bf16)


def finish(ds, one, two, proj, scale):
    high, low = split(jnp.concatenate([ds * two, ds * one], axis=0))
    both = jnp.concatenate([proj, proj], axis=0)
    return dot(jnp.concatenate([high, low], axis=0), both, ((0,), (0,))) * scale


def pack_totals(column, lanes, depth):
    count = column.shape[0]
    row = column.T[:1]
    rows = []
    for start in range(0, count, lanes):
        piece = row[:, start : start + lanes]
        if piece.shape[1] < lanes:
            piece = jnp.concatenate(
                [piece, jnp.zeros((1, lanes - piece.shape[1]), f32)], axis=1
            )
        rows.append(piece)
    rows.append(jnp.zeros((depth - len(rows), lanes), f32))
    return jnp.concatenate(rows, axis=0)


def unpack_totals(packed, count):
    lanes = packed.shape[1]
    parts = [packed[k : k + 1] for k in range(-(-count // lanes))]
    return jnp.concatenate(parts, axis=1)[:, :count]


def ones_beside(v):
    lane = lax.broadcasted_iota(jnp.int32, v.shape, 1)
    return jnp.concatenate([v, jnp.where(lane == 0, 1.0, 0.0).astype(bf16)], axis=1)


def state_with_totals(wide, lanes, rows):
    packed = pack_totals(wide[:, lanes:], lanes, rows - wide.shape[0])
    return jnp.concatenate([wide[:, :lanes], packed], axis=0)


def main_kernel(
    sq_ref, k_ref, v_ref, g_ref, sign_ref, state_ref, dsq_ref, dsk_ref, dv_ref, out_ref
):
    proj = projector(sign_ref)
    width = proj.shape[0] // 2
    pairs = pair_count(width)
    members = sq_ref.shape[0]
    tokens, lanes = v_ref.shape[1:]
    one, two = sketches(k_ref[0], proj, width)
    skt = jnp.concatenate(split(one * two), axis=0)
    sk_high, sk_low = split((one * two).T)
    v = v_ref[0]
    sqt = jnp.concatenate([sq_ref[m, 0] for m in range(members)], axis=1)
    sq = sqt[:width].astype(f32) + sqt[width:].astype(f32)
    gout = jnp.concatenate([g_ref[m, 0].astype(f32).T for m in range(members)], axis=1)
    feat = pair_features(sq)
    held = state_ref[0].astype(f32)
    state = held[:pairs]
    totals = unpack_totals(held[pairs:], pairs)

    inside = nn(
        jnp.concatenate([sk_high, sk_high, sk_low], axis=1),
        jnp.concatenate([sqt, sqt[:width]], axis=0),
    )
    row = lax.broadcasted_iota(jnp.int32, inside.shape, 0)
    column = lax.rem(lax.broadcasted_iota(jnp.int32, inside.shape, 1), tokens)
    inside = jnp.where(row <= column, inside, 0.0)
    weights = (inside * inside * (1.0 / width**2)).astype(bf16)
    left = jnp.concatenate([v.astype(f32).T, jnp.ones((8, tokens), f32)], axis=0).astype(bf16)
    total_high = totals.astype(bf16).astype(f32)
    total_rows = jnp.concatenate(
        [total_high, totals - total_high, jnp.zeros((6, pairs), f32)], axis=0
    )
    state_rows = doubled(jnp.concatenate([state.T, total_rows], axis=0), width, 1).astype(bf16)
    over = nn(left, weights) + nn(state_rows, feat)
    low_total = nn(state_rows[lanes:], feat)[1:2]
    scale = 1.0 / (1.0 + over[lanes : lanes + 1] + low_total)
    rows = gout * scale
    correction = -jnp.sum(rows * over[:lanes], axis=0, keepdims=True) * scale
    low = rows.astype(bf16)
    dscores = nn(v, low) + correction
    edge = (dscores * inside * (2.0 / width**2)).astype(bf16)
    dsk_both = nt(edge, sqt)
    dsk_ref[0] = dsk_both[:, :width] + dsk_both[:, width:]
    dv_ref[0] = nt(weights, low)

    corr_high = correction.astype(bf16).astype(f32)
    corr_rows = jnp.concatenate(
        [corr_high, correction - corr_high, jnp.zeros((lanes - 2, sq.shape[1]), f32)], axis=0
    ).astype(bf16)
    spread = jnp.concatenate([low, corr_rows], axis=0)
    total_columns = jnp.concatenate(
        [totals, totals, jnp.zeros((lanes - 2, pairs), f32)], axis=0
    ).T
    cotangent = nn(jnp.concatenate([state, total_columns], axis=1).astype(bf16), spread)
    dsq_both = nn(skt, edge)
    dsq = dsq_both[:width] + dsq_both[width:] + pair_back(cotangent, sq)
    for m in range(members):
        dsq_ref[m, 0] = dsq[:, m * tokens : (m + 1) * tokens].astype(bf16)

    wide = nt(feat, spread)
    both = wide[:, lanes:] + pltpu.roll(wide[:, lanes:], lanes - 1, 1)
    kept = jnp.concatenate([wide[:, :lanes], both], axis=1)
    out_ref[0] = state_with_totals(kept, lanes, out_ref.shape[1]).astype(bf16)


def call(kernel, outs, args, **more):
    return pl.pallas_call(
        kernel,
        out_shape=outs,
        compiler_params=pltpu.CompilerParams(vmem_limit_bytes=GRANT),
        **more,
    )(*args)


TEAM = 4
CHUNK = 144


def run_scan(reverse, spread, part, sources, out, targets, scratch, ready, fill, early, late, final):
    (mate, chip, other, run_in, run_out, base_out, base_in, give) = scratch[:8]
    (mate_sems, chip_sems, run_sems, base_sems, give_sems, send_y, recv_y, local) = scratch[8:]
    swaps = len(sources)
    blocks = lax.axis_size("ctx")
    sides = lax.axis_size("head")
    groups = blocks // TEAM
    place = lax.axis_index("ctx")
    side = lax.axis_index("head")
    rank = lax.rem(place, TEAM)
    group = place // TEAM
    x = rank // 2
    core = lax.rem(rank, 2)
    chunks = part.shape[1]
    late_x = (1 - x if reverse else x).astype(f32)
    late_core = (1 - core if reverse else core).astype(f32)
    team = group * TEAM
    core_peer = {"ctx": team + 2 * x + 1 - core}
    chip_peer = {"ctx": team + 2 * (1 - x) + core}
    next_group = group - 1 if reverse else group + 1
    has_next = group > 0 if reverse else group < groups - 1
    has_last = group < groups - 1 if reverse else group > 0

    barrier = pltpu.get_barrier_semaphore()

    def greet(target):
        pl.semaphore_signal(
            barrier, inc=1, device_id=target, device_id_type=pl.DeviceIdType.MESH
        )

    greet(core_peer)
    greet(chip_peer)
    ends = 0
    if groups > 1:
        ends = 2
        greet({"ctx": lax.rem(group + 1, groups) * TEAM + rank})
        greet({"ctx": lax.rem(group + groups - 1, groups) * TEAM + rank})
    for k in range(1, sides):
        greet({"head": lax.rem(side + k, sides)})
    pl.semaphore_wait(barrier, 2 + ends + sides - 1)

    def remote(source, target, send, recv, device):
        return pltpu.make_async_remote_copy(
            src_ref=source,
            dst_ref=target,
            send_sem=send,
            recv_sem=recv,
            device_id=device,
            device_id_type=pl.DeviceIdType.MESH,
        )

    def to_mate(at, c):
        return remote(
            part.at[2 * at + 1 - core, c],
            mate.at[at, c],
            mate_sems.at[0, at, c],
            mate_sems.at[1, at, c],
            core_peer,
        )

    def to_chip(c):
        return remote(
            chip.at[c], other.at[c], chip_sems.at[0, c], chip_sems.at[1, c], chip_peer
        )

    def to_next(c):
        return remote(
            run_out.at[c],
            run_in.at[c],
            run_sems.at[0, c],
            run_sems.at[1, c],
            {"ctx": next_group * TEAM + rank},
        )

    def to_base(c):
        return remote(
            base_out.at[c], base_in.at[c], base_sems.at[0, c], base_sems.at[1, c], chip_peer
        )

    def to_give(at, c, to):
        return remote(
            give.at[at, c],
            out.at[2 * at + to, c],
            give_sems.at[0, at, c],
            give_sems.at[1, at, c],
            core_peer,
        )

    def swap(n, k):
        source, target = sources[n], targets[n]
        to = lax.rem(side + k, sides)
        return remote(
            view(source, to), view_to(target, side), send_y.at[n, k - 1], recv_y.at[n, k - 1],
            {"head": to},
        )

    def view(source, to):
        if spread:
            count = source.shape[1] // sides
            return source.at[:, pl.ds(to * count, count)]
        count = source.shape[0] // sides
        return source.at[pl.ds(to * count, count)]

    def view_to(target, at):
        if spread:
            count = target.shape[0] // sides
            return target.at[pl.ds(at * count, count)]
        count = target.shape[1] // sides
        return target.at[:, pl.ds(at * count, count)]

    def keep(n):
        return pltpu.make_async_copy(view(sources[n], side), view_to(targets[n], side), local.at[n])

    def wide(ref, *at):
        return ref[at].astype(f32)

    def deliver(at, c, base):
        mine, theirs = wide(part, 2 * at + core, c), wide(mate, at, c)
        give[at, c] = (base + mine * (1.0 - late_core)).astype(bf16)
        to_give(at, c, core).start()
        out[2 * at + core, c] = (base + theirs * late_core).astype(bf16)

    def begin(n):
        for k in range(1, sides):
            swap(n, k).start()
        keep(n).start()

    def end(n):
        for k in range(1, sides):
            swap(n, k).wait()
        keep(n).wait()

    for n in range(ready):
        begin(n)
    fill()
    for c in range(chunks):
        to_mate(1 - x, c).start()
        to_mate(x, c).start()

    for c in range(chunks):
        to_mate(1 - x, c).wait_recv()
        chip[c] = (wide(part, 2 * (1 - x) + core, c) + wide(mate, 1 - x, c)).astype(bf16)
        to_chip(c).start()

    passed = groups - 1 - group if reverse else group

    def first_part():
        early()
        for n in range(ready, swaps):
            begin(n)

    @pl.when(passed >= 1)
    def _():
        first_part()

    @pl.when(passed >= 2)
    def _():
        late(end)

    for c in range(chunks):
        to_mate(x, c).wait_recv()
        to_chip(c).wait_recv()
        here = wide(part, rank, c) + wide(mate, x, c)
        there = wide(other, c)

        @pl.when(has_last)
        def _():
            to_next(c).wait_recv()

        @pl.when(jnp.logical_not(has_last))
        def _():
            run_in[c] = jnp.zeros_like(run_in[c])

        before = wide(run_in, c)
        run_out[c] = (before + here + there).astype(bf16)

        @pl.when(has_next)
        def _():
            to_next(c).start()

        base_out[c] = (before + here * (1.0 - late_x)).astype(bf16)
        to_base(c).start()
        deliver(x, c, before + there * late_x)

    @pl.when(passed < 1)
    def _():
        first_part()

    @pl.when(passed < 2)
    def _():
        late(end)

    for c in range(chunks):
        to_base(c).wait_recv()
        deliver(1 - x, c, wide(base_in, c))

    final(end)
    for c in range(chunks):
        for at in (x, 1 - x):
            to_give(at, c, 1 - core).wait_recv()
            to_give(at, c, core).wait_send()
            to_mate(at, c).wait_send()
        to_chip(c).wait_send()
        to_base(c).wait_send()

        @pl.when(has_next)
        def _():
            to_next(c).wait_send()


def piece_of(buffer, h, j, per):
    at = h * per + j
    return at // buffer.shape[1], lax.rem(at, buffer.shape[1])


def first_kernel(q_ref, k_ref, v_ref, g_ref, sign_ref, out, s_out, g_out, part, s_held, *scratch):
    proj = projector(sign_ref)
    width = proj.shape[0] // 2
    owned = k_ref.shape[0]
    per = part.shape[0] * part.shape[1] // owned
    rows = part.shape[2]

    def fill():
        @pl.loop(0, owned)
        def _(h):
            one, two = sketches(k_ref[h], proj, width)
            v = v_ref[h]
            wide = nn(pair_features(one * two), ones_beside(v))
            state = state_with_totals(wide, v.shape[1], per * rows).astype(bf16)
            for j in range(per):
                part[piece_of(part, h, j, per)] = state[j * rows : (j + 1) * rows]

    def early():
        @pl.loop(0, q_ref.shape[0])
        def _(m):
            @pl.loop(0, q_ref.shape[1])
            def _(h):
                one, two = sketches(q_ref[m, h], proj, width)
                s_held[m, h] = jnp.concatenate(split(one * two), axis=0)

    run_scan(
        False, True, part, (g_ref, s_held), out, (g_out, s_out), scratch, 1, fill, early,
        lambda end: None,
        lambda end: (end(0), end(1)),
    )


def last_kernel(
    part, q_ref, ds_ref, k_ref, v_ref, sign_ref, dsk_ref, dv_ref, dq_ref, dk_ref, dvo_ref,
    state_ref, ds_all, *scratch,
):
    proj = projector(sign_ref)
    width = proj.shape[0] // 2
    pairs = pair_count(width)
    owned = k_ref.shape[0]
    per = part.shape[0] * part.shape[1] // owned
    inverse = k_ref.shape[-1] ** (-0.5)
    side = lax.axis_index("head")
    mine, heads = q_ref.shape[:2]

    def query_gradient(m, h, ds):
        one, two = sketches(q_ref[m, h], proj, width)
        dq_ref[m, h] = finish(ds.astype(f32), one, two, proj, inverse).astype(bf16)

    def early():
        @pl.loop(0, mine)
        def _(m):
            @pl.loop(0, owned)
            def _(h):
                query_gradient(m, side * owned + h, ds_ref[side * mine + m, h])

    def late(end):
        end(0)

        @pl.loop(0, mine)
        def _(m):
            @pl.loop(owned, heads)
            def _(k):
                h = lax.rem(side * owned + k, heads)
                query_gradient(m, h, ds_all[m, h])

    run_scan(
        True, False, part, (ds_ref,), state_ref, (ds_all,), scratch, 1,
        lambda: None, early, late, lambda end: None,
    )

    @pl.loop(0, owned)
    def _(h):
        one, two = sketches(k_ref[h], proj, width)
        s = one * two
        feat = pair_features(s)
        v = v_ref[h]
        lanes = v.shape[1]
        held = jnp.concatenate(
            [state_ref[piece_of(part, h, j, per)] for j in range(per)], axis=0
        ).astype(f32)
        state = held[:pairs]
        totals = unpack_totals(held[pairs:], pairs)
        total_columns = jnp.concatenate([totals, jnp.zeros((lanes - 1, pairs), f32)], axis=0).T
        cotangent = nt(
            jnp.concatenate([state, total_columns], axis=1).astype(bf16), ones_beside(v)
        )
        ds = dsk_ref[h].T + pair_back(cotangent, s)
        dk_ref[h] = finish(ds, one, two, proj, inverse).astype(bf16)
        state_rows = doubled(state.T, width, 1).astype(bf16)
        dvo_ref[h] = (dv_ref[h] + nn(state_rows, feat).T).astype(bf16)


def pieces(heads, rows, lanes):
    piece = heads * rows // TEAM
    chunks = piece // CHUNK if piece % CHUNK == 0 else 1
    return (TEAM, chunks, piece // chunks, lanes)


def scan_scratch(shape, swaps):
    sides = max(lax.axis_size("head") - 1, 1)
    chunks = shape[1]
    sems = pltpu.SemaphoreType.DMA
    one = pltpu.VMEM(shape[1:], bf16)
    two = pltpu.VMEM((2,) + shape[1:], bf16)
    return [
        two, one, one, one, one, one, one, two,
        sems((2, 2, chunks)),
        sems((2, chunks)),
        sems((2, chunks)),
        sems((2, chunks)),
        sems((2, 2, chunks)),
        sems((swaps, sides)),
        sems((swaps, sides)),
        sems((swaps,)),
    ]


def call_scan(kernel, outs, in_specs, out_specs, scratch, number, args):
    return pl.pallas_call(
        kernel,
        out_shape=outs,
        in_specs=in_specs,
        out_specs=out_specs,
        scratch_shapes=scratch,
        compiler_params=pltpu.CompilerParams(
            collective_id=number, has_side_effects=True, vmem_limit_bytes=GRANT
        ),
    )(*args)


def body(queries, keys, values, dout, signs):
    sign_rows = signs.transpose(0, 2, 1).reshape(-1, signs.shape[1])
    width = signs.shape[-1]
    pairs = pair_count(width)
    rows = -(-(pairs + 16) // CHUNK) * CHUNK
    heads_all = keys.shape[1]
    owned = heads_all // lax.axis_size("head")
    offset = lax.axis_index("head") * owned
    k = lax.dynamic_slice_in_dim(keys.transpose(1, 0, 2), offset, owned, 0)
    v = lax.dynamic_slice_in_dim(values.transpose(1, 0, 2), offset, owned, 0)
    q = queries.transpose(1, 2, 0, 3)
    g = dout.transpose(1, 2, 0, 3)
    mine, _, tokens, hd = q.shape
    members = mine * lax.axis_size("head")
    shape = jax.ShapeDtypeStruct
    shape_in = pieces(owned, rows, hd)
    whole = pl.BlockSpec(memory_space=pltpu.VMEM)
    apart = pl.BlockSpec(memory_space=pl.ANY)
    state, sq, g = call_scan(
        first_kernel,
        (
            shape(shape_in, bf16),
            shape((members, owned, 2 * width, tokens), bf16),
            shape((members, owned, tokens, hd), bf16),
        ),
        [whole, whole, whole, apart, whole],
        (whole, apart, apart),
        [pltpu.VMEM(shape_in, bf16), pltpu.VMEM((mine, heads_all, 2 * width, tokens), bf16)]
        + scan_scratch(shape_in, 2),
        0,
        (q, k, v, g, sign_rows),
    )
    state = state.reshape(owned, rows, hd)
    by_member = lambda h: (0, h, 0, 0)
    by_head = lambda h: (h, 0, 0)
    dsq, dsk, dv, part = call(
        main_kernel,
        (
            shape((members, owned, width, tokens), bf16),
            shape((owned, tokens, width), f32),
            shape((owned, tokens, hd), f32),
            shape((owned, rows, hd), bf16),
        ),
        (sq, k, v, g, sign_rows, state),
        grid=(owned,),
        in_specs=[
            pl.BlockSpec((members, 1, 2 * width, tokens), by_member),
            pl.BlockSpec((1, tokens, hd), by_head),
            pl.BlockSpec((1, tokens, hd), by_head),
            pl.BlockSpec((members, 1, tokens, hd), by_member),
            pl.BlockSpec((2 * width, hd), lambda h: (0, 0)),
            pl.BlockSpec((1, rows, hd), by_head),
        ],
        out_specs=(
            pl.BlockSpec((members, 1, width, tokens), by_member),
            pl.BlockSpec((1, tokens, width), by_head),
            pl.BlockSpec((1, tokens, hd), by_head),
            pl.BlockSpec((1, rows, hd), by_head),
        ),
    )
    dq, dk, dv = call_scan(
        last_kernel,
        (
            shape((mine, heads_all, tokens, hd), bf16),
            shape((owned, tokens, hd), bf16),
            shape((owned, tokens, hd), bf16),
        ),
        [whole] * 8,
        (whole,) * 3,
        [pltpu.VMEM(shape_in, bf16), pltpu.VMEM((mine, heads_all, width, tokens), bf16)]
        + scan_scratch(shape_in, 1),
        1,
        (part.reshape(shape_in), q, dsq, k, v, sign_rows, dsk, dv),
    )
    return dq.transpose(2, 0, 1, 3), dk.transpose(1, 0, 2), dv.transpose(1, 0, 2)


def solution(mesh):
    in_specs = (
        P("ctx", "head", None, None),
        P("ctx", None, None),
        P("ctx", None, None),
        P("ctx", "head", None, None),
        P(),
    )
    out_specs = (P("ctx", "head", None, None), P("ctx", "head", None), P("ctx", "head", None))
    return jax.shard_map(body, mesh=mesh, in_specs=in_specs, out_specs=out_specs, check_vma=False)
```
